256 devices in a mesh: row: 16 (over y, x), col: 16 (over z, core).
Axes of the slice: x: 4, y: 4, z: 8, core: 2. Of those that a mesh axis runs over, the one named last changes fastest.
Arguments:
- queries: bfloat16 [2, 256, 256, 2240], P(None, 'row', 'col'), may hold values from -6 to 6
- key_rows_per_head: bfloat16 [2, 256, 256, 2240], P(None, 'row', 'col'), may hold values from -1000 to 1000
- value_rows_per_head: bfloat16 [2, 256, 256, 2240], P(None, 'row', 'col'), may hold values from -13 to 13
- latent_projection_weight: bfloat16 [2240, 32], replicated, may hold values from -0.125 to 0.125
- entry_conv_weight: bfloat16 [3, 3, 32, 512], replicated, may hold values from -0.375 to 0.375
- residual_norm_gain: float32 [512], replicated, may hold values from 0.1 to 1.9
- residual_conv_weight: bfloat16 [3, 3, 512, 512], replicated, may hold values from -0.09375 to 0.09375
- upscale_conv_weight: bfloat16 [3, 3, 512, 512], replicated, may hold values from -0.09375 to 0.09375
Outputs:
- decoded_image: bfloat16 [2, 512, 512, 512], P(None, 'row', 'col')
The draws below stay inside these ranges and needn't reach their ends.
All inputs are finite; a program needn't handle non-finite values.
Results may differ from the reference program's by a relative error of at most 0.017.
Values may be sent and summed in bfloat16 or wider, within the bound.
No kernel may reach another device: no remote copies, remote signals or barrier semaphores. Data moves between devices by JAX's collectives and lax.ppermute only.
A program may use at most 128 MiB of HBM per device.

```python
import jax
import jax.numpy as jnp
from jax import lax

HEADS = 70
HEAD = 32
MODEL_WIDTH = 2240
LATENT_CHANNELS = 32
HALF_CHANNELS = 512
C_UP = 512
TILE = 16
IMAGES = 2
TOKEN_ROWS = 256
TOKEN_COLUMNS = 256


def common_draws(key):
    normal_part = jnp.clip(jax.random.normal(key, (IMAGES, TOKEN_ROWS, TOKEN_COLUMNS, MODEL_WIDTH), jnp.float32), -4.0, 4.0)
    return normal_part


def spatial_ramp():
    row_pos = jnp.arange(TOKEN_ROWS, dtype=jnp.float32) / (TOKEN_ROWS - 1)
    col_pos = jnp.arange(TOKEN_COLUMNS, dtype=jnp.float32) / (TOKEN_COLUMNS - 1)
    return (1.0 + 2.0 * row_pos)[:, None] * (1.0 + 2.0 * col_pos)[None, :] / 3.0


def token_scales(key, low, high):
    logs = jax.random.uniform(key, (IMAGES, TOKEN_ROWS, TOKEN_COLUMNS, 1), jnp.float32, jnp.log(low), jnp.log(high))
    return jnp.exp(logs)


def tile_weights(key):
    tile_rows = TOKEN_ROWS // TILE
    tile_cols = TOKEN_COLUMNS // TILE
    tile_count = tile_rows * tile_cols
    heavy_count = max(1, tile_count // 32)
    order = jax.random.permutation(key, tile_count)
    heavy = (order < heavy_count).reshape(tile_rows, tile_cols)
    factor = jnp.where(heavy, 16.0, 1.0).astype(jnp.float32)
    factor = jnp.repeat(jnp.repeat(factor, TILE, axis=0), TILE, axis=1)
    return factor[None, :, :, None]


def draw_key_rows_per_head(key, part):
    normal_part = common_draws(key)
    key = jax.random.fold_in(key, 11)
    heavy = tile_weights(jax.random.fold_in(key, 5))
    base = normal_part
    scales = token_scales(key, 0.5, 5.0)
    return (base * scales * heavy * spatial_ramp()[None, :, :, None]).astype(jnp.bfloat16)


def draw_value_rows_per_head(key, part):
    normal_part = common_draws(key)
    key = jax.random.fold_in(key, 23)
    base = normal_part
    keys_all = jax.random.split(key, 6)
    grouped = base.reshape(IMAGES, TOKEN_ROWS, TOKEN_COLUMNS, HEADS, HEAD)
    first_gain = jax.random.uniform(keys_all[0], (HEADS, HEAD), jnp.float32, 0.3, 1.0)
    second_gain = jax.random.uniform(keys_all[1], (HEADS, HEAD), jnp.float32, -0.6, 0.6)
    third_gain = jax.random.uniform(keys_all[2], (HEADS, HEAD), jnp.float32, -0.6, 0.6)
    mixed = first_gain * grouped + second_gain * jnp.roll(grouped, -1, axis=-1) + third_gain * jnp.roll(grouped, -5, axis=-1)
    row_slope = jax.random.uniform(keys_all[3], (MODEL_WIDTH,), jnp.float32, -1.0, 1.0)
    col_slope = jax.random.uniform(keys_all[4], (MODEL_WIDTH,), jnp.float32, -1.0, 1.0)
    row_pos = 2.0 * jnp.arange(TOKEN_ROWS, dtype=jnp.float32) / (TOKEN_ROWS - 1) - 1.0
    col_pos = 2.0 * jnp.arange(TOKEN_COLUMNS, dtype=jnp.float32) / (TOKEN_COLUMNS - 1) - 1.0
    trend = row_slope * row_pos[:, None, None] + col_slope * col_pos[None, :, None]
    noise = 0.5 * jnp.clip(jax.random.normal(keys_all[5], (IMAGES, TOKEN_ROWS, TOKEN_COLUMNS, MODEL_WIDTH), jnp.float32), -4.0, 4.0)
    return (mixed.reshape(IMAGES, TOKEN_ROWS, TOKEN_COLUMNS, MODEL_WIDTH) + trend[None] + noise).astype(jnp.bfloat16)


def shard_levels(key, extent, cuts, low, high):
    def one(axis_at, parts):
        draws = jax.random.uniform(jax.random.fold_in(jax.random.fold_in(key, 6), axis_at), (parts,), jnp.float32, low / len(cuts), high / len(cuts))
        return jnp.repeat(jnp.exp(draws), extent[axis_at] // parts).reshape((-1,) + (1,) * (len(extent) - axis_at - 1))

    gain = one(*cuts[0])
    for cut in cuts[1:]:
        gain = gain * one(*cut)
    return gain


def normal_values(key, dims, deviation, most, shards=(), kind=jnp.bfloat16):
    level = shard_levels(key, dims, shards, -0.22, 0.18) if shards else 1.0
    result = jax.random.normal(key, dims, jnp.float32) * deviation * level
    return jnp.minimum(jnp.maximum(result, -most), most).astype(kind)


def setup_inputs(seed: int = 0) -> dict:
    key_list = jax.random.split(jax.random.key(seed), 9)
    return {
        "queries": normal_values(key_list[0], (IMAGES, TOKEN_ROWS, TOKEN_COLUMNS, MODEL_WIDTH), 1.0, 6.0, ((1, 16), (2, 16))),
        "key_rows_per_head": draw_key_rows_per_head(jax.random.fold_in(key_list[8], 71), 0),
        "value_rows_per_head": draw_value_rows_per_head(jax.random.fold_in(key_list[8], 71), 0),
        "latent_projection_weight": normal_values(key_list[3], (MODEL_WIDTH, LATENT_CHANNELS), MODEL_WIDTH ** -0.5, 0.125),
        "entry_conv_weight": normal_values(key_list[4], (3, 3, LATENT_CHANNELS, HALF_CHANNELS), (9 * LATENT_CHANNELS) ** -0.5, 0.375),
        "residual_norm_gain": jnp.clip(1.0 + 0.18 * jax.random.normal(key_list[5], (HALF_CHANNELS,), jnp.float32), 0.1, 1.9),
        "residual_conv_weight": normal_values(key_list[6], (3, 3, HALF_CHANNELS, HALF_CHANNELS), (9 * HALF_CHANNELS) ** -0.5, 0.09375),
        "upscale_conv_weight": normal_values(key_list[7], (3, 3, HALF_CHANNELS, C_UP), (9 * HALF_CHANNELS) ** -0.5, 0.09375),
    }


NORM_EPS = 1e-06

def convolve_padded(inputs, weights):
    return lax.conv_general_dilated(inputs.astype(jnp.float32), weights.astype(jnp.float32), (1, 1), ((1, 1), (1, 1)), dimension_numbers=('NHWC', 'HWIO', 'NHWC'))

def activate(decoder_output, residual_norm_gain):
    values_f = decoder_output.astype(jnp.float32)
    scaled = values_f * lax.rsqrt(lax.optimization_barrier(jnp.mean(values_f * values_f, axis=-1, keepdims=True)) + NORM_EPS) * residual_norm_gain.astype(jnp.float32)
    return jax.nn.silu(scaled).astype(jnp.bfloat16)

def attend_image(query_img, key_img, value_img, latent_projection_weight):
    token_count = TOKEN_ROWS * TOKEN_COLUMNS
    relu_keys = jnp.maximum(key_img.astype(jnp.float32), 0.0).reshape(token_count, HEADS, HEAD)
    head_values = value_img.astype(jnp.float32).reshape(token_count, HEADS, HEAD)
    key_value = jnp.einsum('nhi,nhj->hij', relu_keys, head_values) / token_count
    key_mean = lax.optimization_barrier(jnp.sum(relu_keys, axis=0)) / token_count
    key_value = lax.optimization_barrier(key_value.astype(jnp.bfloat16)).astype(jnp.float32)
    key_mean = lax.optimization_barrier(key_mean.astype(jnp.bfloat16)).astype(jnp.float32)
    relu_query = jnp.maximum(query_img.astype(jnp.float32), 0.0).reshape(token_count, HEADS, HEAD)
    numerator = jnp.einsum('nhi,hij->nhj', relu_query, key_value)
    denominator = jnp.einsum('nhi,hi->nh', relu_query, key_mean)
    attended = (numerator / jnp.maximum(denominator, 1.0)[:, :, None]).reshape(token_count, MODEL_WIDTH)
    normed = (attended * lax.rsqrt(lax.optimization_barrier(jnp.mean(attended * attended, axis=1, keepdims=True)) + NORM_EPS)).astype(jnp.bfloat16)
    latent_state = jnp.dot(normed, latent_projection_weight, preferred_element_type=jnp.float32).astype(jnp.bfloat16)
    return latent_state.reshape(TOKEN_ROWS, TOKEN_COLUMNS, LATENT_CHANNELS)

def reference(queries, key_rows_per_head, value_rows_per_head, latent_projection_weight, entry_conv_weight, residual_norm_gain, residual_conv_weight, upscale_conv_weight):
    latent_state = lax.map(lambda operands: attend_image(operands[0], operands[1], operands[2], latent_projection_weight), (queries, key_rows_per_head, value_rows_per_head))
    decoder_output = convolve_padded(latent_state, entry_conv_weight).astype(jnp.bfloat16)
    hidden_state = activate(decoder_output, residual_norm_gain)
    residual_output = (decoder_output.astype(jnp.float32) + convolve_padded(hidden_state, residual_conv_weight)).astype(jnp.bfloat16)
    upsampled = jnp.repeat(jnp.repeat(residual_output, 2, axis=1), 2, axis=2)
    return convolve_padded(upsampled, upscale_conv_weight).astype(jnp.bfloat16)
```

```python
import functools

import jax
import jax.numpy as jnp
from jax import lax
from jax.experimental import pallas as pl
from jax.experimental.pallas import tpu as pltpu
from jax.sharding import PartitionSpec as P

HEAD = 32
NORM_EPS = 1e-06
LANES = 128
PACK = 2560
KS_AT = 2304


def sums_kernel(scale, _, k_ref, v_ref, out_ref):
    tokens, width = k_ref.shape[1:]
    ones = jnp.ones((tokens, LANES), jnp.bfloat16)
    lane = lax.broadcasted_iota(jnp.int32, (HEAD, LANES), 1)
    parts = []
    key_sums = jnp.zeros((HEAD, LANES), jnp.float32)
    for start in range(0, width, LANES):
        size = min(LANES, width - start)
        keys = jnp.maximum(k_ref[0, :, start : start + size], 0)
        values = jnp.concatenate([v_ref[0, :, start : start + size], ones], axis=1)
        product = lax.dot_general(
            keys, values, (((0,), (0,)), ((), ())), preferred_element_type=jnp.float32
        )
        packed = jnp.zeros((HEAD, size), jnp.float32)
        for h in range(size // HEAD):
            rows = product[h * HEAD : (h + 1) * HEAD]
            packed = jnp.where(lane[:, :size] // HEAD == h, rows[:, :size], packed)
            key_sums = jnp.where(lane == start // HEAD + h, rows[:, size:], key_sums)
        parts.append(packed)
    parts.append(jnp.zeros((HEAD, KS_AT - width), jnp.float32))
    parts.append(key_sums)
    parts.append(jnp.zeros((HEAD, PACK - KS_AT - LANES), jnp.float32))
    total = (jnp.concatenate(parts, axis=1) * scale).astype(jnp.bfloat16)
    half = PACK // 2
    for r in range(2):
        for c in range(2):
            out_ref[2 * r + c] = total[16 * r : 16 * r + 16, half * c : half * (c + 1)]


def image_sums(keys, values, image, scale):
    images, tokens, width = keys.shape
    spec = pl.BlockSpec((1, tokens, width), lambda i, at: (at[0], 0, 0))
    return pl.pallas_call(
        functools.partial(sums_kernel, scale),
        out_shape=jax.ShapeDtypeStruct((4, 16, PACK // 2), jnp.bfloat16),
        grid_spec=pltpu.PrefetchScalarGridSpec(
            num_scalar_prefetch=1,
            grid=(1,),
            in_specs=[spec, spec],
            out_specs=pl.BlockSpec((4, 16, PACK // 2), lambda i, at: (0, 0, 0)),
        ),
        compiler_params=pltpu.CompilerParams(vmem_limit_bytes=32 << 20),
        cost_estimate=pl.CostEstimate(flops=2 * tokens * width * 256, bytes_accessed=4 * tokens * width, transcendentals=0),
        name="image_sums",
    )(image.reshape(1), keys, values)


def attend_kernel(q_ref, kv_ref, w_ref, out_ref):
    tokens, width = q_ref.shape[1:]
    group = 2 * LANES
    same = (
        lax.broadcasted_iota(jnp.int32, (group, group), 0) // HEAD
        == lax.broadcasted_iota(jnp.int32, (group, group), 1) // HEAD
    )
    kv = jnp.concatenate(
        [jnp.concatenate([kv_ref[0, 2 * r + c] for c in range(2)], axis=1) for r in range(2)], axis=0
    )
    key_means = kv[:, KS_AT : KS_AT + LANES]
    head_of = lax.broadcasted_iota(jnp.int32, (LANES, group), 0)
    lane_head = lax.broadcasted_iota(jnp.int32, (LANES, group), 1) // HEAD
    squares = jnp.zeros((tokens, 1), jnp.float32)
    latent = jnp.zeros((tokens, w_ref.shape[1]), jnp.float32)
    for start in range(0, width, group):
        size = min(group, width - start)
        spread = (head_of == lane_head + start // HEAD).astype(jnp.bfloat16)[:, :size]
        means = jnp.dot(key_means, spread, preferred_element_type=jnp.float32).astype(jnp.bfloat16)
        here = same[:size, :size]
        zero = jnp.zeros((size, size), jnp.bfloat16)
        numerator_weights = jnp.where(
            here, jnp.concatenate([kv[:, start : start + size]] * (size // HEAD), axis=0), zero
        )
        denominator_weights = jnp.where(
            here, jnp.concatenate([means] * (size // HEAD), axis=0), zero
        )
        query = jnp.maximum(q_ref[0, :, start : start + size], 0)
        numerator = jnp.dot(query, numerator_weights, preferred_element_type=jnp.float32)
        denominator = jnp.dot(query, denominator_weights, preferred_element_type=jnp.float32)
        bound = jnp.maximum(denominator, 1.0)
        inverse = pl.reciprocal(bound, approx=True)
        attended = numerator * (inverse * (2.0 - bound * inverse))
        squares += jnp.sum(attended * attended, axis=1, keepdims=True)
        latent += jnp.dot(
            attended.astype(jnp.bfloat16),
            w_ref[start : start + size],
            preferred_element_type=jnp.float32,
        )
    out_ref[0] = (latent * lax.rsqrt(squares / width + NORM_EPS)).astype(jnp.bfloat16)


def attend(queries, kv, weight):
    images, tokens, width = queries.shape
    channels = weight.shape[1]
    return pl.pallas_call(
        attend_kernel,
        out_shape=jax.ShapeDtypeStruct((images, tokens, channels), jnp.bfloat16),
        grid=(images,),
        in_specs=[
            pl.BlockSpec((1, tokens, width), lambda i: (i, 0, 0)),
            pl.BlockSpec((1, 4, 16, PACK // 2), lambda i: (i, 0, 0, 0)),
            pl.BlockSpec((width, channels), lambda i: (0, 0)),
        ],
        out_specs=pl.BlockSpec((1, tokens, channels), lambda i: (i, 0, 0)),
        compiler_params=pltpu.CompilerParams(vmem_limit_bytes=32 << 20),
        cost_estimate=pl.CostEstimate(flops=2 * images * tokens * width * 512, bytes_accessed=2 * images * tokens * width, transcendentals=0),
        name="attend",
    )(queries, kv, weight)


def xor_pairs(distance):
    return [(i, i ^ distance) for i in range(16)]


def exchange_group(value, axis, distances):
    arrived = [lax.ppermute(value, axis, xor_pairs(d)) for d in distances]
    total = value.astype(jnp.float32)
    for part in arrived:
        total = total + part.astype(jnp.float32)
    return total.astype(jnp.bfloat16)


def sum_over_mesh(mine, other):
    at_x = lax.axis_index("row") % 4
    core = lax.axis_index("col") % 2
    arrived = lax.ppermute(other, "col", xor_pairs(1))
    image = mine.astype(jnp.float32) + arrived.astype(jnp.float32)
    parts = [
        lax.ppermute(
            lax.dynamic_index_in_dim(image, at_x ^ d, 0, False).astype(jnp.bfloat16), "row", xor_pairs(d)
        )
        for d in (1, 3, 2)
    ]
    total = lax.dynamic_index_in_dim(image, at_x, 0, False)
    for part in parts:
        total = total + part.astype(jnp.float32)
    chunk = exchange_group(total.astype(jnp.bfloat16), "row", (4, 12, 8))
    chunk = exchange_group(chunk, "col", (2,))
    chunk = exchange_group(chunk, "col", (4, 12, 10))
    twin = lax.ppermute(chunk, "col", xor_pairs(1))
    both = jnp.where(core == 0, jnp.stack([chunk, twin]), jnp.stack([twin, chunk]))
    gathered = jnp.stack([both] + [lax.ppermute(both, "row", xor_pairs(d)) for d in (1, 2, 3)])
    return jnp.stack(
        [lax.dynamic_index_in_dim(gathered, at_x ^ c, 0, False) for c in range(4)], axis=1
    )


def extended(value, sides, width):
    for axis, dim in sides:
        devices, length = (lax.axis_size(axis), value.shape[dim])
        up = [(i, (i + 1) % devices) for i in range(devices - 1)]
        down = [(j, i) for i, j in up]
        last = lax.slice_in_dim(value, length - width, length, axis=dim)
        initial = lax.slice_in_dim(value, 0, width, axis=dim)
        before = lax.ppermute(last, axis, up)
        after = lax.ppermute(initial, axis, down)
        value = jnp.concatenate([before, value, after], axis=dim)
    return value


def convolve_unpadded(inputs, weights):
    return lax.conv_general_dilated(
        inputs,
        weights,
        (1, 1),
        "VALID",
        dimension_numbers=("NHWC", "HWIO", "NHWC"),
        preferred_element_type=jnp.float32,
    )


def activate(decoder_output, residual_norm_gain):
    values_f = decoder_output.astype(jnp.float32)
    scaled = (
        values_f
        * lax.rsqrt(jnp.mean(values_f * values_f, axis=-1, keepdims=True) + NORM_EPS)
        * residual_norm_gain
    )
    return jax.nn.silu(scaled)


def inside(tile, margin):
    marks = []
    for axis in ("row", "col"):
        at = lax.axis_index(axis) * tile - margin + jnp.arange(tile + 2 * margin)
        marks.append((at >= 0) & (at < tile * lax.axis_size(axis)))
    return (marks[0][:, None] & marks[1][None, :])[None, :, :, None]


def upsample(residual_output):
    return jnp.repeat(jnp.repeat(residual_output, 2, axis=1), 2, axis=2)


def local(
    queries,
    key_rows_per_head,
    value_rows_per_head,
    latent_projection_weight,
    entry_conv_weight,
    residual_norm_gain,
    residual_conv_weight,
    upscale_conv_weight,
):
    images, tile, _, width = queries.shape
    scale = 1.0 / (tile * lax.axis_size("row") * tile * lax.axis_size("col"))
    flat = (images, tile * tile, width)
    keys, values = key_rows_per_head.reshape(flat), value_rows_per_head.reshape(flat)
    core = (lax.axis_index("col") % 2).astype(jnp.int32)
    other = image_sums(keys, values, 1 - core, scale)
    mine = image_sums(keys, values, core, scale)
    kv = sum_over_mesh(mine, other)
    latent = attend(queries.reshape(flat), kv, latent_projection_weight)
    latent = latent.reshape(images, tile, tile, latent.shape[-1])
    widened = extended(latent, (("row", 1), ("col", 2)), 3)
    decoded = convolve_unpadded(widened, entry_conv_weight).astype(jnp.bfloat16)
    hidden = jnp.where(inside(tile, 2), activate(decoded, residual_norm_gain), 0).astype(jnp.bfloat16)
    refined = decoded[:, 1:-1, 1:-1].astype(jnp.float32) + convolve_unpadded(hidden, residual_conv_weight)
    refined = jnp.where(inside(tile, 1), refined, 0).astype(jnp.bfloat16)
    upsampled = upsample(refined)[:, 1:-1, 1:-1, :]
    return convolve_unpadded(upsampled, upscale_conv_weight).astype(jnp.bfloat16)


def solution(mesh):
    placed = (
        P(None, "row", "col", None),
        P(None, "row", "col", None),
        P(None, "row", "col", None),
        P(),
        P(),
        P(),
        P(),
        P(),
    )
    return jax.shard_map(
        local, mesh=mesh, in_specs=placed, out_specs=P(None, "row", "col", None), check_vma=False
    )
```

```python
import functools

import jax
import jax.numpy as jnp
from jax import lax
from jax.experimental import pallas as pl
from jax.experimental.pallas import tpu as pltpu
from jax.sharding import PartitionSpec as P

HEAD = 32
NORM_EPS = 1e-06
LANES = 128
PACK = 2560
KS_AT = 2304


def sums_kernel(scale, _, k_ref, v_ref, out_ref):
    tokens, width = k_ref.shape[1:]
    ones = jnp.ones((tokens, LANES), jnp.bfloat16)
    lane = lax.broadcasted_iota(jnp.int32, (HEAD, LANES), 1)
    parts = []
    key_sums = jnp.zeros((HEAD, LANES), jnp.float32)
    for start in range(0, width, LANES):
        size = min(LANES, width - start)
        keys = jnp.maximum(k_ref[0, :, start : start + size], 0)
        values = jnp.concatenate([v_ref[0, :, start : start + size], ones], axis=1)
        product = lax.dot_general(
            keys, values, (((0,), (0,)), ((), ())), preferred_element_type=jnp.float32
        )
        packed = jnp.zeros((HEAD, size), jnp.float32)
        for h in range(size // HEAD):
            rows = product[h * HEAD : (h + 1) * HEAD]
            packed = jnp.where(lane[:, :size] // HEAD == h, rows[:, :size], packed)
            key_sums = jnp.where(lane == start // HEAD + h, rows[:, size:], key_sums)
        parts.append(packed)
    parts.append(jnp.zeros((HEAD, KS_AT - width), jnp.float32))
    parts.append(key_sums)
    parts.append(jnp.zeros((HEAD, PACK - KS_AT - LANES), jnp.float32))
    total = (jnp.concatenate(parts, axis=1) * scale).astype(jnp.bfloat16)
    half = PACK // 2
    for r in range(2):
        for c in range(2):
            out_ref[2 * r + c] = total[16 * r : 16 * r + 16, half * c : half * (c + 1)]


def image_sums(keys, values, image, scale):
    images, tokens, width = keys.shape
    spec = pl.BlockSpec((1, tokens, width), lambda i, at: (at[0], 0, 0))
    return pl.pallas_call(
        functools.partial(sums_kernel, scale),
        out_shape=jax.ShapeDtypeStruct((4, 16, PACK // 2), jnp.bfloat16),
        grid_spec=pltpu.PrefetchScalarGridSpec(
            num_scalar_prefetch=1,
            grid=(1,),
            in_specs=[spec, spec],
            out_specs=pl.BlockSpec((4, 16, PACK // 2), lambda i, at: (0, 0, 0)),
        ),
        compiler_params=pltpu.CompilerParams(vmem_limit_bytes=32 << 20),
        cost_estimate=pl.CostEstimate(flops=2 * tokens * width * 256, bytes_accessed=4 * tokens * width, transcendentals=0),
        name="image_sums",
    )(image.reshape(1), keys, values)


def attend_kernel(q_ref, kv_ref, w_ref, out_ref):
    tokens, width = q_ref.shape[1:]
    group = 2 * LANES
    same = (
        lax.broadcasted_iota(jnp.int32, (group, group), 0) // HEAD
        == lax.broadcasted_iota(jnp.int32, (group, group), 1) // HEAD
    )
    kv = jnp.concatenate(
        [jnp.concatenate([kv_ref[0, 2 * r + c] for c in range(2)], axis=1) for r in range(2)], axis=0
    )
    key_means = kv[:, KS_AT : KS_AT + LANES]
    head_of = lax.broadcasted_iota(jnp.int32, (LANES, group), 0)
    lane_head = lax.broadcasted_iota(jnp.int32, (LANES, group), 1) // HEAD
    squares = jnp.zeros((tokens, 1), jnp.float32)
    latent = jnp.zeros((tokens, w_ref.shape[1]), jnp.float32)
    for start in range(0, width, group):
        size = min(group, width - start)
        spread = (head_of == lane_head + start // HEAD).astype(jnp.bfloat16)[:, :size]
        means = jnp.dot(key_means, spread, preferred_element_type=jnp.float32).astype(jnp.bfloat16)
        here = same[:size, :size]
        zero = jnp.zeros((size, size), jnp.bfloat16)
        numerator_weights = jnp.where(
            here, jnp.concatenate([kv[:, start : start + size]] * (size // HEAD), axis=0), zero
        )
        denominator_weights = jnp.where(
            here, jnp.concatenate([means] * (size // HEAD), axis=0), zero
        )
        query = jnp.maximum(q_ref[0, :, start : start + size], 0)
        numerator = jnp.dot(query, numerator_weights, preferred_element_type=jnp.float32)
        denominator = jnp.dot(query, denominator_weights, preferred_element_type=jnp.float32)
        bound = jnp.maximum(denominator, 1.0)
        inverse = pl.reciprocal(bound, approx=True)
        attended = numerator * (inverse * (2.0 - bound * inverse))
        squares += jnp.sum(attended * attended, axis=1, keepdims=True)
        latent += jnp.dot(
            attended.astype(jnp.bfloat16),
            w_ref[start : start + size],
            preferred_element_type=jnp.float32,
        )
    out_ref[0] = (latent * lax.rsqrt(squares / width + NORM_EPS)).astype(jnp.bfloat16)


def attend(queries, kv, weight):
    images, tokens, width = queries.shape
    channels = weight.shape[1]
    return pl.pallas_call(
        attend_kernel,
        out_shape=jax.ShapeDtypeStruct((images, tokens, channels), jnp.bfloat16),
        grid=(images,),
        in_specs=[
            pl.BlockSpec((1, tokens, width), lambda i: (i, 0, 0)),
            pl.BlockSpec((1, 4, 16, PACK // 2), lambda i: (i, 0, 0, 0)),
            pl.BlockSpec((width, channels), lambda i: (0, 0)),
        ],
        out_specs=pl.BlockSpec((1, tokens, channels), lambda i: (i, 0, 0)),
        compiler_params=pltpu.CompilerParams(vmem_limit_bytes=32 << 20),
        cost_estimate=pl.CostEstimate(flops=2 * images * tokens * width * 512, bytes_accessed=2 * images * tokens * width, transcendentals=0),
        name="attend",
    )(queries, kv, weight)


def xor_pairs(distance):
    return [(i, i ^ distance) for i in range(16)]


def exchange_group(value, axis, distances):
    arrived = [lax.ppermute(value, axis, xor_pairs(d)) for d in distances]
    total = value.astype(jnp.float32)
    for part in arrived:
        total = total + part.astype(jnp.float32)
    return total.astype(jnp.bfloat16)


def sum_over_mesh(mine, other):
    at_x = lax.axis_index("row") % 4
    core = lax.axis_index("col") % 2
    arrived = lax.ppermute(other, "col", xor_pairs(1))
    image = mine.astype(jnp.float32) + arrived.astype(jnp.float32)
    parts = [
        lax.ppermute(
            lax.dynamic_index_in_dim(image, at_x ^ d, 0, False).astype(jnp.bfloat16), "row", xor_pairs(d)
        )
        for d in (1, 3, 2)
    ]
    total = lax.dynamic_index_in_dim(image, at_x, 0, False)
    for part in parts:
        total = total + part.astype(jnp.float32)
    chunk = exchange_group(total.astype(jnp.bfloat16), "row", (4, 12, 8))
    chunk = exchange_group(chunk, "col", (2,))
    chunk = exchange_group(chunk, "col", (4, 12, 10))
    twin = lax.ppermute(chunk, "col", xor_pairs(1))
    both = jnp.where(core == 0, jnp.stack([chunk, twin]), jnp.stack([twin, chunk]))
    gathered = jnp.stack([both] + [lax.ppermute(both, "row", xor_pairs(d)) for d in (1, 2, 3)])
    return jnp.stack(
        [lax.dynamic_index_in_dim(gathered, at_x ^ c, 0, False) for c in range(4)], axis=1
    )


def extended(value, sides, width):
    for axis, dim in sides:
        devices, length = (lax.axis_size(axis), value.shape[dim])
        up = [(i, (i + 1) % devices) for i in range(devices - 1)]
        down = [(j, i) for i, j in up]
        last = lax.slice_in_dim(value, length - width, length, axis=dim)
        initial = lax.slice_in_dim(value, 0, width, axis=dim)
        before = lax.ppermute(last, axis, up)
        after = lax.ppermute(initial, axis, down)
        value = jnp.concatenate([before, value, after], axis=dim)
    return value


def read(ref, at):
    return jnp.concatenate([ref[c, at, :] for c in range(ref.shape[0])], axis=1)


def write(ref, at, value):
    for c in range(ref.shape[0]):
        ref[c, at, :] = value[:, LANES * c : LANES * (c + 1)]


def decode_kernel(
    tiles, at_ref, lat_ref, entry_ref, gain_ref, residual_ref, upscale_ref, out_ref,
    wide, dec, hid, taps, ref, centre, slope, mix,
):
    tile = 16
    channels = out_ref.shape[-1]
    pitch = 24
    f32, bf16 = jnp.float32, jnp.bfloat16
    rows = tile + 4
    spot = lax.broadcasted_iota(jnp.int32, (2 * pitch, 1), 0) % pitch

    def real(at, axis):
        return (at >= 0) & (at < tile * tiles[axis])

    for i in range(2 * (tile + 6)):
        block = [lat_ref[i, dx : dx + pitch, :] for dx in range(3)]
        wide[pitch * i : pitch * (i + 1)] = jnp.concatenate(block, axis=1).astype(bf16)

    across = real(at_ref[1] * tile - 2 + spot, 1)
    gain = gain_ref[...]
    for y in range(rows):
        at = 2 * pitch * y
        value = jnp.dot(wide[at : at + 2 * pitch], entry_ref[0], preferred_element_type=f32)
        for dy in (1, 2):
            start = at + 2 * pitch * dy
            value += jnp.dot(wide[start : start + 2 * pitch], entry_ref[dy], preferred_element_type=f32)
        value = value.astype(bf16).astype(f32)
        write(dec, pl.ds(at, 2 * pitch), value)
        mean = jnp.mean(value * value, axis=1, keepdims=True)
        scaled = value * lax.rsqrt(mean + NORM_EPS) * gain
        active = 0.5 * scaled * (1.0 + jnp.tanh(0.5 * scaled))
        keep = across & real(at_ref[0] * tile - 2 + y, 0)
        write(hid, pl.ds(at, 2 * pitch), jnp.where(keep, active, 0.0))
    spare = jnp.zeros((8 * pitch, channels), f32)
    write(hid, pl.ds(2 * pitch * rows, 8 * pitch), spare)
    write(dec, pl.ds(2 * pitch * rows, 8 * pitch), spare)

    inner = 2 * (tile + 2)
    main = inner * tile
    edge = 40
    for i in range(2 * rows):
        for dx in range(3):
            piece = read(hid, pl.ds(pitch * i + dx, tile)).astype(bf16)
            for dy in range(3):
                j = i - 2 * dy
                if 0 <= j < inner:
                    tap = (3 * dy + dx) * channels
                    taps[tile * j : tile * (j + 1), tap : tap + channels] = piece
    for dy in range(3):
        for x in range(tile, tile + 4):
            piece = read(hid, pl.ds(2 * pitch * dy + x, edge, stride=pitch)).astype(bf16)
            for e in range(2):
                dx = x - tile - e
                if 0 <= dx < 3:
                    tap = (3 * dy + dx) * channels
                    taps[main + edge * e : main + edge * (e + 1), tap : tap + channels] = piece

    conv = jnp.dot(taps[...], residual_ref[...], preferred_element_type=f32)
    column = real(at_ref[1] * tile - 1 + lax.broadcasted_iota(jnp.int32, (tile, 1), 0), 1)
    for i in range(inner):
        value = conv[tile * i : tile * (i + 1)] + read(dec, pl.ds(pitch * (i + 2) + 1, tile))
        keep = column & real(at_ref[0] * tile - 1 + i // 2, 0)
        write(ref, pl.ds(pitch * i, tile), jnp.where(keep, value, 0.0).astype(bf16).astype(f32))
    line = real(at_ref[0] * tile - 1 + lax.broadcasted_iota(jnp.int32, (edge, 1), 0) // 2, 0)
    for e in range(2):
        value = conv[main + edge * e : main + edge * (e + 1)]
        value += read(dec, pl.ds(2 * pitch + tile + 1 + e, edge, stride=pitch))
        keep = line & real(at_ref[1] * tile - 1 + tile + e, 1)
        value = jnp.where(keep, value, 0.0).astype(bf16).astype(f32)
        write(ref, pl.ds(tile + e, edge, stride=pitch), value)

    def column_parts(i):
        left, here, right = (read(ref, pl.ds(pitch * i + d, tile)) for d in range(3))
        return left - here, here, right - here

    for image in range(2):
        before = column_parts(image)
        for y in range(tile + 1):
            after = column_parts(2 * (y + 1) + image)
            at = tile * (2 * y + image)
            for q in range(3):
                slope[q, at : at + tile] = (before[q] - after[q]).astype(bf16)
                if y < tile:
                    centre[q, at : at + tile] = after[q].astype(bf16)
            before = after

    total = 2 * tile * tile

    def product(p, q):
        source = centre[q] if p == 1 else slope[q, tile * p : tile * p + total]
        return jnp.dot(source, upscale_ref[3 * p + q], preferred_element_type=f32)

    middle = product(1, 1)
    shared = (middle + product(1, 0), middle + product(1, 2))
    for a in range(2):
        between = product(2 * a, 1)
        for b in range(2):
            value = shared[b] + between + product(2 * a, 2 * b)
            write(mix.at[a], pl.ds(b, total, stride=2), value)
    for y in range(tile):
        for image in range(2):
            at = 2 * tile * (2 * y + image)
            for a in range(2):
                out_ref[image, 2 * y + a] = read(mix.at[a], pl.ds(at, 2 * tile)).astype(bf16)


def phases_kernel(w_ref, out_ref):
    wide = [w_ref[t].astype(jnp.float32) for t in range(9)]
    down = [
        [wide[q], wide[q] + wide[3 + q] + wide[6 + q], -wide[6 + q]] for q in range(3)
    ]
    for p in range(3):
        parts = [down[q][p] for q in range(3)]
        out_ref[3 * p] = parts[0].astype(jnp.bfloat16)
        out_ref[3 * p + 1] = (parts[0] + parts[1] + parts[2]).astype(jnp.bfloat16)
        out_ref[3 * p + 2] = parts[2].astype(jnp.bfloat16)


def phases(upscale):
    deep, channels = upscale.shape[2:]
    block = pl.BlockSpec((9, deep // 4, channels), lambda i: (0, i, 0))
    return pl.pallas_call(
        phases_kernel,
        out_shape=jax.ShapeDtypeStruct((9, deep, channels), jnp.bfloat16),
        grid=(4,),
        in_specs=[block],
        out_specs=block,
        compiler_params=pltpu.CompilerParams(vmem_limit_bytes=24 << 20),
        cost_estimate=pl.CostEstimate(flops=10 * deep * channels, bytes_accessed=36 * deep * channels, transcendentals=0),
        name="phases",
    )(upscale.reshape(9, deep, channels))


def decode(at, latent, entry, gain, residual, u, tiles):
    images, tile = latent.shape[0], 16
    channels = entry.shape[-1]
    pitch = 24
    padded = jnp.pad(latent, ((0, 0), (0, 0), (0, 10), (0, 0))).astype(jnp.float32)
    padded = padded.transpose(1, 0, 2, 3).reshape(images * (tile + 6), 32, latent.shape[-1])
    rows = images * (tile + 4) + 8
    inner = images * (tile + 2)
    total = images * tile * tile
    f32, bf16 = jnp.float32, jnp.bfloat16
    vmem = pl.BlockSpec(memory_space=pltpu.VMEM)
    return pl.pallas_call(
        functools.partial(decode_kernel, tiles),
        out_shape=jax.ShapeDtypeStruct((images, 2 * tile, 2 * tile, channels), bf16),
        in_specs=[pl.BlockSpec(memory_space=pltpu.SMEM)] + [vmem] * 5,
        out_specs=vmem,
        scratch_shapes=[
            pltpu.VMEM((images * (tile + 6) * pitch, 3 * latent.shape[-1]), bf16),
            pltpu.VMEM((channels // LANES, rows * pitch, LANES), f32),
            pltpu.VMEM((channels // LANES, rows * pitch, LANES), f32),
            pltpu.VMEM((inner * tile + 80, 9 * channels), bf16),
            pltpu.VMEM((channels // LANES, (inner + 4) * pitch, LANES), f32),
            pltpu.VMEM((3, total, channels), bf16),
            pltpu.VMEM((3, total + images * tile, channels), bf16),
            pltpu.VMEM((2, channels // LANES, 2 * total, LANES), f32),
        ],
        compiler_params=pltpu.CompilerParams(vmem_limit_bytes=44 << 20),
        cost_estimate=pl.CostEstimate(flops=8 * 10**9, bytes_accessed=12 << 20, transcendentals=0),
        name="decode",
    )(
        at,
        padded,
        entry.reshape(3, 3 * entry.shape[2], channels),
        gain.reshape(1, channels),
        residual.reshape(9 * channels, channels),
        u,
    )


def local(
    queries,
    key_rows_per_head,
    value_rows_per_head,
    latent_projection_weight,
    entry_conv_weight,
    residual_norm_gain,
    residual_conv_weight,
    upscale_conv_weight,
):
    images, tile, _, width = queries.shape
    scale = 1.0 / (tile * lax.axis_size("row") * tile * lax.axis_size("col"))
    flat = (images, tile * tile, width)
    keys, values = key_rows_per_head.reshape(flat), value_rows_per_head.reshape(flat)
    core = (lax.axis_index("col") % 2).astype(jnp.int32)
    other = image_sums(keys, values, 1 - core, scale)
    mine = image_sums(keys, values, core, scale)
    kv = sum_over_mesh(mine, other)
    latent = attend(queries.reshape(flat), kv, latent_projection_weight)
    latent = latent.reshape(images, tile, tile, latent.shape[-1])
    widened = extended(latent, (("row", 1), ("col", 2)), 3)
    at = jnp.stack([lax.axis_index("row"), lax.axis_index("col")]).astype(jnp.int32)
    tiles = (lax.axis_size("row"), lax.axis_size("col"))
    return decode(
        at,
        widened,
        entry_conv_weight,
        residual_norm_gain,
        residual_conv_weight,
        phases(upscale_conv_weight),
        tiles,
    )


def solution(mesh):
    placed = (
        P(None, "row", "col", None),
        P(None, "row", "col", None),
        P(None, "row", "col", None),
        P(),
        P(),
        P(),
        P(),
        P(),
    )
    return jax.shard_map(
        local, mesh=mesh, in_specs=placed, out_specs=P(None, "row", "col", None), check_vma=False
    )
```

```python
import functools

import jax
import jax.numpy as jnp
from jax import lax
from jax.experimental import pallas as pl
from jax.experimental.pallas import tpu as pltpu
from jax.sharding import PartitionSpec as P

HEAD = 32
NORM_EPS = 1e-06
LANES = 128
PACK = 2560
KS_AT = 2304


def sums_kernel(scale, core_ref, k_hbm, v_hbm, mine_ref, other_ref, k_ref, v_ref, sems):
    images, tokens, width = k_ref.shape
    core = core_ref[0]
    half = tokens // 2
    copies = []
    for n in range(images):
        image = 1 - core if n == 0 else core
        for c in range(2):
            at = pl.ds(half * c, half)
            for m, (source, target) in enumerate(((k_hbm, k_ref), (v_hbm, v_ref))):
                copies.append(
                    pltpu.make_async_copy(source.at[image, at], target.at[n, at], sems.at[n, c, m])
                )
    for copy in copies:
        copy.start()
    ones = jnp.ones((tokens, LANES), jnp.bfloat16)
    lane = lax.broadcasted_iota(jnp.int32, (HEAD, LANES), 1)
    for n, out_ref in ((0, other_ref), (1, mine_ref)):
        for copy in copies[4 * n : 4 * n + 4]:
            copy.wait()
        parts = []
        key_sums = jnp.zeros((HEAD, LANES), jnp.float32)
        for start in range(0, width, LANES):
            size = min(LANES, width - start)
            keys = jnp.maximum(k_ref[n, :, start : start + size], 0)
            values = jnp.concatenate([v_ref[n, :, start : start + size], ones], axis=1)
            product = lax.dot_general(
                keys, values, (((0,), (0,)), ((), ())), preferred_element_type=jnp.float32
            )
            packed = jnp.zeros((HEAD, size), jnp.float32)
            for h in range(size // HEAD):
                rows = product[h * HEAD : (h + 1) * HEAD]
                packed = jnp.where(lane[:, :size] // HEAD == h, rows[:, :size], packed)
                key_sums = jnp.where(lane == start // HEAD + h, rows[:, size:], key_sums)
            parts.append(packed)
        parts.append(jnp.zeros((HEAD, KS_AT - width), jnp.float32))
        parts.append(key_sums)
        parts.append(jnp.zeros((HEAD, PACK - KS_AT - LANES), jnp.float32))
        total = (jnp.concatenate(parts, axis=1) * scale).astype(jnp.bfloat16)
        wide = PACK // 2
        for r in range(2):
            for c in range(2):
                out_ref[2 * r + c] = total[16 * r : 16 * r + 16, wide * c : wide * (c + 1)]


def image_sums(keys, values, core, scale):
    images, tokens, width = keys.shape
    out = jax.ShapeDtypeStruct((4, 16, PACK // 2), jnp.bfloat16)
    vmem = pl.BlockSpec(memory_space=pltpu.VMEM)
    hbm = pl.BlockSpec(memory_space=pl.ANY)
    return pl.pallas_call(
        functools.partial(sums_kernel, scale),
        out_shape=[out, out],
        in_specs=[pl.BlockSpec(memory_space=pltpu.SMEM), hbm, hbm],
        out_specs=[vmem, vmem],
        scratch_shapes=[
            pltpu.VMEM(keys.shape, keys.dtype),
            pltpu.VMEM(values.shape, values.dtype),
            pltpu.SemaphoreType.DMA((images, 2, 2)),
        ],
        compiler_params=pltpu.CompilerParams(vmem_limit_bytes=58 << 20),
        cost_estimate=pl.CostEstimate(flops=4 * tokens * width * 256, bytes_accessed=8 * tokens * width, transcendentals=0),
        name="image_sums",
    )(core.reshape(1), keys, values)


def attend_kernel(q_ref, kv_ref, w_ref, out_ref):
    tokens, width = q_ref.shape[1:]
    group = 2 * LANES
    same = (
        lax.broadcasted_iota(jnp.int32, (group, group), 0) // HEAD
        == lax.broadcasted_iota(jnp.int32, (group, group), 1) // HEAD
    )
    kv = jnp.concatenate(
        [jnp.concatenate([kv_ref[0, 2 * r + c] for c in range(2)], axis=1) for r in range(2)], axis=0
    )
    key_means = kv[:, KS_AT : KS_AT + LANES]
    head_of = lax.broadcasted_iota(jnp.int32, (LANES, group), 0)
    lane_head = lax.broadcasted_iota(jnp.int32, (LANES, group), 1) // HEAD
    squares = jnp.zeros((tokens, 1), jnp.float32)
    latent = jnp.zeros((tokens, w_ref.shape[1]), jnp.float32)
    for start in range(0, width, group):
        size = min(group, width - start)
        spread = (head_of == lane_head + start // HEAD).astype(jnp.bfloat16)[:, :size]
        means = jnp.dot(key_means, spread, preferred_element_type=jnp.float32).astype(jnp.bfloat16)
        here = same[:size, :size]
        zero = jnp.zeros((size, size), jnp.bfloat16)
        numerator_weights = jnp.where(
            here, jnp.concatenate([kv[:, start : start + size]] * (size // HEAD), axis=0), zero
        )
        denominator_weights = jnp.where(
            here, jnp.concatenate([means] * (size // HEAD), axis=0), zero
        )
        query = jnp.maximum(q_ref[0, :, start : start + size], 0)
        numerator = jnp.dot(query, numerator_weights, preferred_element_type=jnp.float32)
        denominator = jnp.dot(query, denominator_weights, preferred_element_type=jnp.float32)
        bound = jnp.maximum(denominator, 1.0)
        inverse = pl.reciprocal(bound, approx=True)
        attended = numerator * (inverse * (2.0 - bound * inverse))
        squares += jnp.sum(attended * attended, axis=1, keepdims=True)
        latent += jnp.dot(
            attended.astype(jnp.bfloat16),
            w_ref[start : start + size],
            preferred_element_type=jnp.float32,
        )
    out_ref[0] = (latent * lax.rsqrt(squares / width + NORM_EPS)).astype(jnp.bfloat16)


def attend(queries, kv, weight):
    images, tokens, width = queries.shape
    channels = weight.shape[1]
    return pl.pallas_call(
        attend_kernel,
        out_shape=jax.ShapeDtypeStruct((images, tokens, channels), jnp.bfloat16),
        grid=(images,),
        in_specs=[
            pl.BlockSpec((1, tokens, width), lambda i: (i, 0, 0)),
            pl.BlockSpec((1, 4, 16, PACK // 2), lambda i: (i, 0, 0, 0)),
            pl.BlockSpec((width, channels), lambda i: (0, 0)),
        ],
        out_specs=pl.BlockSpec((1, tokens, channels), lambda i: (i, 0, 0)),
        compiler_params=pltpu.CompilerParams(vmem_limit_bytes=24 << 20),
        cost_estimate=pl.CostEstimate(flops=2 * images * tokens * width * 512, bytes_accessed=2 * images * tokens * width, transcendentals=0),
        name="attend",
    )(queries, kv, weight)


def xor_pairs(distance):
    return [(i, i ^ distance) for i in range(16)]


def exchange_group(value, axis, distances):
    arrived = [lax.ppermute(value, axis, xor_pairs(d)) for d in distances]
    total = value.astype(jnp.float32)
    for part in arrived:
        total = total + part.astype(jnp.float32)
    return total.astype(jnp.bfloat16)


def sum_over_mesh(mine, other, upscale):
    at_x = lax.axis_index("row") % 4
    core = lax.axis_index("col") % 2
    arrived = lax.ppermute(other, "col", xor_pairs(1))
    image = mine.astype(jnp.float32) + arrived.astype(jnp.float32)
    parts = [
        lax.ppermute(
            lax.dynamic_index_in_dim(image, at_x ^ d, 0, False).astype(jnp.bfloat16), "row", xor_pairs(d)
        )
        for d in (1, 3, 2)
    ]
    total = lax.dynamic_index_in_dim(image, at_x, 0, False)
    for part in parts:
        total = total + part.astype(jnp.float32)
    chunk = exchange_group(total.astype(jnp.bfloat16), "row", (4, 12, 8))
    chunk = exchange_group(chunk, "col", (2,))
    chunk, upscale = lax.optimization_barrier((chunk, upscale))
    arrived = [lax.ppermute(chunk, "col", xor_pairs(d)) for d in (4, 12, 10)]
    arrived, combined = lax.optimization_barrier((arrived, phases(upscale)))
    total = chunk.astype(jnp.float32)
    for part in arrived:
        total = total + part.astype(jnp.float32)
    chunk = total.astype(jnp.bfloat16)
    twin = lax.ppermute(chunk, "col", xor_pairs(1))
    both = jnp.where(core == 0, jnp.stack([chunk, twin]), jnp.stack([twin, chunk]))
    gathered = jnp.stack([both] + [lax.ppermute(both, "row", xor_pairs(d)) for d in (1, 2, 3)])
    whole = jnp.stack(
        [lax.dynamic_index_in_dim(gathered, at_x ^ c, 0, False) for c in range(4)], axis=1
    )
    return whole, combined


def extended(value, sides, width):
    for axis, dim in sides:
        devices, length = (lax.axis_size(axis), value.shape[dim])
        up = [(i, (i + 1) % devices) for i in range(devices - 1)]
        down = [(j, i) for i, j in up]
        last = lax.slice_in_dim(value, length - width, length, axis=dim)
        initial = lax.slice_in_dim(value, 0, width, axis=dim)
        before = lax.ppermute(last, axis, up)
        after = lax.ppermute(initial, axis, down)
        value = jnp.concatenate([before, value, after], axis=dim)
    return value


def read(ref, at):
    return jnp.concatenate([ref[c, at, :] for c in range(ref.shape[0])], axis=1)


def write(ref, at, value):
    for c in range(ref.shape[0]):
        ref[c, at, :] = value[:, LANES * c : LANES * (c + 1)]


def decode_kernel(
    tiles, at_ref, lat_ref, entry_ref, gain_ref, residual_ref, upscale_ref, out_hbm,
    wide, dec, hid, taps, ref, centre, slope, mix, out_ref, sems,
):
    tile = 16
    channels = out_hbm.shape[-1]
    pitch = 24
    f32, bf16 = jnp.float32, jnp.bfloat16
    rows = tile + 4
    spot = lax.broadcasted_iota(jnp.int32, (2 * pitch, 1), 0) % pitch

    def real(at, axis):
        return (at >= 0) & (at < tile * tiles[axis])

    for i in range(2 * (tile + 6)):
        block = [lat_ref[i, dx : dx + pitch, :] for dx in range(3)]
        wide[pitch * i : pitch * (i + 1)] = jnp.concatenate(block, axis=1).astype(bf16)

    across = real(at_ref[1] * tile - 2 + spot, 1)
    gain = gain_ref[...]
    for y in range(rows):
        at = 2 * pitch * y
        value = jnp.dot(wide[at : at + 2 * pitch], entry_ref[0], preferred_element_type=f32)
        for dy in (1, 2):
            start = at + 2 * pitch * dy
            value += jnp.dot(wide[start : start + 2 * pitch], entry_ref[dy], preferred_element_type=f32)
        value = value.astype(bf16).astype(f32)
        write(dec, pl.ds(at, 2 * pitch), value)
        mean = jnp.mean(value * value, axis=1, keepdims=True)
        scaled = value * lax.rsqrt(mean + NORM_EPS) * gain
        active = 0.5 * scaled * (1.0 + jnp.tanh(0.5 * scaled))
        keep = across & real(at_ref[0] * tile - 2 + y, 0)
        write(hid, pl.ds(at, 2 * pitch), jnp.where(keep, active, 0.0))
    spare = jnp.zeros((8 * pitch, channels), f32)
    write(hid, pl.ds(2 * pitch * rows, 8 * pitch), spare)
    write(dec, pl.ds(2 * pitch * rows, 8 * pitch), spare)

    inner = 2 * (tile + 2)
    main = inner * tile
    edge = 40
    for i in range(2 * rows):
        for dx in range(3):
            piece = read(hid, pl.ds(pitch * i + dx, tile)).astype(bf16)
            for dy in range(3):
                j = i - 2 * dy
                if 0 <= j < inner:
                    tap = (3 * dy + dx) * channels
                    taps[tile * j : tile * (j + 1), tap : tap + channels] = piece
    for dy in range(3):
        for x in range(tile, tile + 4):
            piece = read(hid, pl.ds(2 * pitch * dy + x, edge, stride=pitch)).astype(bf16)
            for e in range(2):
                dx = x - tile - e
                if 0 <= dx < 3:
                    tap = (3 * dy + dx) * channels
                    taps[main + edge * e : main + edge * (e + 1), tap : tap + channels] = piece

    conv = jnp.dot(taps[...], residual_ref[...], preferred_element_type=f32)
    column = real(at_ref[1] * tile - 1 + lax.broadcasted_iota(jnp.int32, (tile, 1), 0), 1)
    for i in range(inner):
        value = conv[tile * i : tile * (i + 1)] + read(dec, pl.ds(pitch * (i + 2) + 1, tile))
        keep = column & real(at_ref[0] * tile - 1 + i // 2, 0)
        write(ref, pl.ds(pitch * i, tile), jnp.where(keep, value, 0.0).astype(bf16).astype(f32))
    line = real(at_ref[0] * tile - 1 + lax.broadcasted_iota(jnp.int32, (edge, 1), 0) // 2, 0)
    for e in range(2):
        value = conv[main + edge * e : main + edge * (e + 1)]
        value += read(dec, pl.ds(2 * pitch + tile + 1 + e, edge, stride=pitch))
        keep = line & real(at_ref[1] * tile - 1 + tile + e, 1)
        value = jnp.where(keep, value, 0.0).astype(bf16).astype(f32)
        write(ref, pl.ds(tile + e, edge, stride=pitch), value)

    def column_parts(i):
        left, here, right = (read(ref, pl.ds(pitch * i + d, tile)) for d in range(3))
        return left - here, here, right - here

    for image in range(2):
        before = column_parts(image)
        for y in range(tile + 1):
            after = column_parts(2 * (y + 1) + image)
            at = tile * (2 * y + image)
            for q in range(3):
                slope[q, at : at + tile] = (before[q] - after[q]).astype(bf16)
                if y < tile:
                    centre[q, at : at + tile] = after[q].astype(bf16)
            before = after

    total = 2 * tile * tile

    def product(p, q):
        source = centre[q] if p == 1 else slope[q, tile * p : tile * p + total]
        return jnp.dot(source, upscale_ref[3 * p + q], preferred_element_type=f32)

    middle = product(1, 1)
    stores = []
    shared = (middle + product(1, 0), middle + product(1, 2))
    for a in range(2):
        between = product(2 * a, 1)
        for b in range(2):
            value = shared[b] + between + product(2 * a, 2 * b)
            write(mix.at[a], pl.ds(b, total, stride=2), value)
        for y in range(tile):
            for image in range(2):
                at = 2 * tile * (2 * y + image)
                out_ref[a, image, y] = read(mix.at[a], pl.ds(at, 2 * tile)).astype(bf16)
        stores.append(pltpu.make_async_copy(out_ref.at[a], out_hbm.at[:, :, a], sems.at[a]))
        stores[a].start()
    for store in stores:
        store.wait()


def phases_kernel(w_ref, out_ref):
    wide = [w_ref[t].astype(jnp.float32) for t in range(9)]
    down = [
        [wide[q], wide[q] + wide[3 + q] + wide[6 + q], -wide[6 + q]] for q in range(3)
    ]
    for p in range(3):
        parts = [down[q][p] for q in range(3)]
        out_ref[3 * p] = parts[0].astype(jnp.bfloat16)
        out_ref[3 * p + 1] = (parts[0] + parts[1] + parts[2]).astype(jnp.bfloat16)
        out_ref[3 * p + 2] = parts[2].astype(jnp.bfloat16)


def phases(upscale):
    deep, channels = upscale.shape[2:]
    block = pl.BlockSpec((9, deep // 4, channels), lambda i: (0, i, 0))
    return pl.pallas_call(
        phases_kernel,
        out_shape=jax.ShapeDtypeStruct((9, deep, channels), jnp.bfloat16),
        grid=(4,),
        in_specs=[block],
        out_specs=block,
        compiler_params=pltpu.CompilerParams(vmem_limit_bytes=24 << 20),
        cost_estimate=pl.CostEstimate(flops=10 * deep * channels, bytes_accessed=36 * deep * channels, transcendentals=0),
        name="phases",
    )(upscale.reshape(9, deep, channels))


def decode(at, latent, entry, gain, residual, u, tiles):
    images, tile = latent.shape[0], 16
    channels = entry.shape[-1]
    pitch = 24
    padded = jnp.pad(latent, ((0, 0), (0, 0), (0, 10), (0, 0))).astype(jnp.float32)
    padded = padded.transpose(1, 0, 2, 3).reshape(images * (tile + 6), 32, latent.shape[-1])
    rows = images * (tile + 4) + 8
    inner = images * (tile + 2)
    total = images * tile * tile
    f32, bf16 = jnp.float32, jnp.bfloat16
    vmem = pl.BlockSpec(memory_space=pltpu.VMEM)
    out = pl.pallas_call(
        functools.partial(decode_kernel, tiles),
        out_shape=jax.ShapeDtypeStruct((images, tile, 2, 2 * tile, channels), bf16),
        in_specs=[pl.BlockSpec(memory_space=pltpu.SMEM)] + [vmem] * 5,
        out_specs=pl.BlockSpec(memory_space=pl.ANY),
        scratch_shapes=[
            pltpu.VMEM((images * (tile + 6) * pitch, 3 * latent.shape[-1]), bf16),
            pltpu.VMEM((channels // LANES, rows * pitch, LANES), f32),
            pltpu.VMEM((channels // LANES, rows * pitch, LANES), f32),
            pltpu.VMEM((inner * tile + 80, 9 * channels), bf16),
            pltpu.VMEM((channels // LANES, (inner + 4) * pitch, LANES), f32),
            pltpu.VMEM((3, total, channels), bf16),
            pltpu.VMEM((3, total + images * tile, channels), bf16),
            pltpu.VMEM((2, channels // LANES, 2 * total, LANES), f32),
            pltpu.VMEM((2, images, tile, 2 * tile, channels), bf16),
            pltpu.SemaphoreType.DMA((2,)),
        ],
        compiler_params=pltpu.CompilerParams(vmem_limit_bytes=38 << 20),
        cost_estimate=pl.CostEstimate(flops=8 * 10**9, bytes_accessed=12 << 20, transcendentals=0),
        name="decode",
    )(
        at,
        padded,
        entry.reshape(3, 3 * entry.shape[2], channels),
        gain.reshape(1, channels),
        residual.reshape(9 * channels, channels),
        u,
    )
    return out.reshape(images, 2 * tile, 2 * tile, channels)


def local(
    queries,
    key_rows_per_head,
    value_rows_per_head,
    latent_projection_weight,
    entry_conv_weight,
    residual_norm_gain,
    residual_conv_weight,
    upscale_conv_weight,
):
    images, tile, _, width = queries.shape
    scale = 1.0 / (tile * lax.axis_size("row") * tile * lax.axis_size("col"))
    flat = (images, tile * tile, width)
    keys, values = key_rows_per_head.reshape(flat), value_rows_per_head.reshape(flat)
    core = (lax.axis_index("col") % 2).astype(jnp.int32)
    mine, other = image_sums(keys, values, core, scale)
    kv, combined = sum_over_mesh(mine, other, upscale_conv_weight)
    latent = attend(queries.reshape(flat), kv, latent_projection_weight)
    latent = latent.reshape(images, tile, tile, latent.shape[-1])
    widened = extended(latent, (("row", 1), ("col", 2)), 3)
    at = jnp.stack([lax.axis_index("row"), lax.axis_index("col")]).astype(jnp.int32)
    tiles = (lax.axis_size("row"), lax.axis_size("col"))
    return decode(
        at,
        widened,
        entry_conv_weight,
        residual_norm_gain,
        residual_conv_weight,
        combined,
        tiles,
    )


def solution(mesh):
    placed = (
        P(None, "row", "col", None),
        P(None, "row", "col", None),
        P(None, "row", "col", None),
        P(),
        P(),
        P(),
        P(),
        P(),
    )
    return jax.shard_map(
        local, mesh=mesh, in_specs=placed, out_specs=P(None, "row", "col", None), check_vma=False
    )
```

```python
import functools

import jax
import jax.numpy as jnp
from jax import lax
from jax.experimental import pallas as pl
from jax.experimental.pallas import tpu as pltpu
from jax.sharding import PartitionSpec as P

HEAD = 32
NORM_EPS = 1e-06
LANES = 128
PACK = 2560
KS_AT = 2304


def sums_kernel(scale, core_ref, k_hbm, v_hbm, mine_ref, other_ref, k_ref, v_ref, sems):
    images, tokens, width = k_ref.shape
    core = core_ref[0]
    half = tokens // 2
    copies = []
    for n in range(images):
        image = 1 - core if n == 0 else core
        for c in range(2):
            at = pl.ds(half * c, half)
            for m, (source, target) in enumerate(((k_hbm, k_ref), (v_hbm, v_ref))):
                copies.append(
                    pltpu.make_async_copy(source.at[image, at], target.at[n, at], sems.at[n, c, m])
                )
    for copy in copies:
        copy.start()
    ones = jnp.ones((tokens, LANES), jnp.bfloat16)
    lane = lax.broadcasted_iota(jnp.int32, (HEAD, LANES), 1)
    for n, out_ref in ((0, other_ref), (1, mine_ref)):
        for copy in copies[4 * n : 4 * n + 4]:
            copy.wait()
        parts = []
        key_sums = jnp.zeros((HEAD, LANES), jnp.float32)
        for start in range(0, width, LANES):
            size = min(LANES, width - start)
            keys = jnp.maximum(k_ref[n, :, start : start + size], 0)
            values = jnp.concatenate([v_ref[n, :, start : start + size], ones], axis=1)
            product = lax.dot_general(
                keys, values, (((0,), (0,)), ((), ())), preferred_element_type=jnp.float32
            )
            packed = jnp.zeros((HEAD, size), jnp.float32)
            for h in range(size // HEAD):
                rows = product[h * HEAD : (h + 1) * HEAD]
                packed = jnp.where(lane[:, :size] // HEAD == h, rows[:, :size], packed)
                key_sums = jnp.where(lane == start // HEAD + h, rows[:, size:], key_sums)
            parts.append(packed)
        parts.append(jnp.zeros((HEAD, KS_AT - width), jnp.float32))
        parts.append(key_sums)
        parts.append(jnp.zeros((HEAD, PACK - KS_AT - LANES), jnp.float32))
        total = (jnp.concatenate(parts, axis=1) * scale).astype(jnp.bfloat16)
        wide = PACK // 2
        for r in range(2):
            for c in range(2):
                out_ref[2 * r + c] = total[16 * r : 16 * r + 16, wide * c : wide * (c + 1)]


def image_sums(keys, values, core, scale):
    images, tokens, width = keys.shape
    out = jax.ShapeDtypeStruct((4, 16, PACK // 2), jnp.bfloat16)
    vmem = pl.BlockSpec(memory_space=pltpu.VMEM)
    hbm = pl.BlockSpec(memory_space=pl.ANY)
    return pl.pallas_call(
        functools.partial(sums_kernel, scale),
        out_shape=[out, out],
        in_specs=[pl.BlockSpec(memory_space=pltpu.SMEM), hbm, hbm],
        out_specs=[vmem, vmem],
        scratch_shapes=[
            pltpu.VMEM(keys.shape, keys.dtype),
            pltpu.VMEM(values.shape, values.dtype),
            pltpu.SemaphoreType.DMA((images, 2, 2)),
        ],
        compiler_params=pltpu.CompilerParams(vmem_limit_bytes=58 << 20),
        cost_estimate=pl.CostEstimate(flops=4 * tokens * width * 256, bytes_accessed=8 * tokens * width, transcendentals=0),
        name="image_sums",
    )(core.reshape(1), keys, values)


def attend_kernel(at_ref, q_ref, piece0_ref, piece1_ref, piece2_ref, piece3_ref, weight_ref, out_ref, sums):
    f32, bf16 = jnp.float32, jnp.bfloat16
    images, tokens, width = q_ref.shape
    group = 2 * LANES
    for n, piece in enumerate((piece0_ref, piece1_ref, piece2_ref, piece3_ref)):
        sums[at_ref[2] ^ n] = piece[...]
    same = (
        lax.broadcasted_iota(jnp.int32, (group, group), 0) // HEAD
        == lax.broadcasted_iota(jnp.int32, (group, group), 1) // HEAD
    )
    same = same.astype(f32).astype(bf16)
    head_of = lax.broadcasted_iota(jnp.int32, (LANES, PACK), 0)
    lane_head = lax.broadcasted_iota(jnp.int32, (LANES, PACK), 1) // HEAD
    spread = (head_of == lane_head).astype(f32).astype(bf16)
    kv = [
        jnp.concatenate(
            [jnp.concatenate([sums[2 * r + c, image] for c in range(2)], axis=1) for r in range(2)], axis=0
        )
        for image in range(images)
    ]
    key_means = jnp.concatenate([part[:, KS_AT : KS_AT + LANES] for part in kv], axis=0)
    means = jnp.dot(key_means, spread, preferred_element_type=f32).astype(bf16)
    squares = [jnp.zeros((tokens, LANES), f32)] * images
    latent = jnp.zeros((images * tokens, weight_ref.shape[0]), f32)
    for start in range(0, width, group):
        size = min(group, width - start)
        repeat = size // HEAD
        here = same[:size, :size]
        parts = []
        for image in range(images):
            upper = kv[image][:, start : start + size]
            lower = means[HEAD * image : HEAD * (image + 1), start : start + size]
            query = jnp.maximum(q_ref[image, :, start : start + size], 0)
            numerator = jnp.dot(
                query, jnp.concatenate([upper] * repeat, axis=0) * here, preferred_element_type=f32
            )
            denominator = jnp.dot(
                query, jnp.concatenate([lower] * repeat, axis=0) * here, preferred_element_type=f32
            )
            attended = numerator * pl.reciprocal(jnp.maximum(denominator, 1.0), approx=True)
            square = attended * attended
            for c in range(0, size, LANES):
                part = square[:, c : min(c + LANES, size)]
                if part.shape[1] < LANES:
                    rest = jnp.zeros((tokens, LANES - part.shape[1]), f32)
                    part = jnp.concatenate([part, rest], axis=1)
                squares[image] += part
            parts.append(attended.astype(bf16))
        latent += lax.dot_general(
            jnp.concatenate(parts, axis=0),
            weight_ref[:, start : start + size],
            (((1,), (1,)), ((), ())),
            preferred_element_type=f32,
        )
    for image in range(images):
        total = jnp.sum(squares[image], axis=1, keepdims=True)
        normed = latent[tokens * image : tokens * (image + 1)] * lax.rsqrt(total / width + NORM_EPS)
        out_ref[image] = normed.astype(bf16)


def attend(at, queries, pieces, weight):
    images, tokens, width = queries.shape
    channels = weight.shape[1]
    vmem = pl.BlockSpec(memory_space=pltpu.VMEM)
    return pl.pallas_call(
        attend_kernel,
        out_shape=jax.ShapeDtypeStruct((images, tokens, channels), jnp.bfloat16),
        in_specs=[pl.BlockSpec(memory_space=pltpu.SMEM)] + [vmem] * 6,
        out_specs=vmem,
        scratch_shapes=[pltpu.VMEM((4, images, 16, PACK // 2), jnp.bfloat16)],
        compiler_params=pltpu.CompilerParams(vmem_limit_bytes=32 << 20),
        cost_estimate=pl.CostEstimate(flops=2 * images * tokens * width * 512, bytes_accessed=2 * images * tokens * width, transcendentals=0),
        name="attend",
    )(at, queries, *pieces, weight.T)


def xor_pairs(distance):
    return [(i, i ^ distance) for i in range(16)]


def added(value, arrived):
    total = value.astype(jnp.float32)
    for part in arrived:
        total = total + part.astype(jnp.float32)
    return total.astype(jnp.bfloat16)


def sent(value, axis, distances):
    return [lax.ppermute(value, axis, xor_pairs(d)) for d in distances]


def gather_all(mine, other, residual, upscale):
    hold = lax.optimization_barrier
    at_x = lax.axis_index("row") % 4
    first = lax.axis_index("col") % 2 == 0
    mine, other, first = hold((mine, other, first))
    arrived = lax.ppermute(other, "col", xor_pairs(1))
    image = mine.astype(jnp.float32) + arrived.astype(jnp.float32)
    parts = [
        lax.ppermute(
            lax.dynamic_index_in_dim(image, at_x ^ d, 0, False).astype(jnp.bfloat16), "row", xor_pairs(d)
        )
        for d in (1, 3, 2)
    ]
    chunk = added(lax.dynamic_index_in_dim(image, at_x, 0, False), parts)

    chunk, weights = hold((chunk, residual))
    arrived = sent(chunk, "row", (4, 12, 8))
    arrived, kept = hold((arrived, keep(weights)))
    chunk = added(chunk, arrived)

    chunk = added(chunk, sent(chunk, "col", (2,)))

    chunk, weights = hold((chunk, upscale))
    arrived = sent(chunk, "col", (4, 12, 10))
    arrived, combined = hold((arrived, phases(weights)))
    chunk = added(chunk, arrived)

    twin = lax.ppermute(chunk, "col", xor_pairs(1))
    both = jnp.where(first, jnp.stack([chunk, twin]), jnp.stack([twin, chunk]))
    pieces = [both] + sent(both, "row", (1, 2, 3))
    return pieces, kept, combined


def extended(value, sides, width):
    for axis, dim in sides:
        devices, length = (lax.axis_size(axis), value.shape[dim])
        up = [(i, (i + 1) % devices) for i in range(devices - 1)]
        down = [(j, i) for i, j in up]
        last = lax.slice_in_dim(value, length - width, length, axis=dim)
        initial = lax.slice_in_dim(value, 0, width, axis=dim)
        before = lax.ppermute(last, axis, up)
        after = lax.ppermute(initial, axis, down)
        value = jnp.concatenate([before, value, after], axis=dim)
    return value


def read(ref, at):
    return jnp.concatenate([ref[c, at, :] for c in range(ref.shape[0])], axis=1)


def write(ref, at, value):
    for c in range(ref.shape[0]):
        ref[c, at, :] = value[:, LANES * c : LANES * (c + 1)]


def decode_kernel(
    tiles, at_ref, lat_ref, entry_ref, gain_ref, residual_ref, upscale_ref, out_hbm,
    wide, dec, hid, taps, ref, centre, slope, mix, out_ref, sems,
):
    tile = 16
    channels = out_hbm.shape[-1]
    pitch = 24
    f32, bf16 = jnp.float32, jnp.bfloat16
    rows = tile + 4
    spot = lax.broadcasted_iota(jnp.int32, (2 * pitch, 1), 0) % pitch

    def real(at, axis):
        return (at >= 0) & (at < tile * tiles[axis])

    for i in range(2 * (tile + 6)):
        block = [lat_ref[i, dx : dx + pitch, :] for dx in range(3)]
        wide[pitch * i : pitch * (i + 1)] = jnp.concatenate(block, axis=1).astype(bf16)

    across = real(at_ref[1] * tile - 2 + spot, 1)
    gain = gain_ref[...]
    for y in range(rows):
        at = 2 * pitch * y
        value = jnp.dot(wide[at : at + 2 * pitch], entry_ref[0], preferred_element_type=f32)
        for dy in (1, 2):
            start = at + 2 * pitch * dy
            value += jnp.dot(wide[start : start + 2 * pitch], entry_ref[dy], preferred_element_type=f32)
        value = value.astype(bf16).astype(f32)
        write(dec, pl.ds(at, 2 * pitch), value)
        mean = jnp.mean(value * value, axis=1, keepdims=True)
        scaled = value * lax.rsqrt(mean + NORM_EPS) * gain
        active = 0.5 * scaled * (1.0 + jnp.tanh(0.5 * scaled))
        keep = across & real(at_ref[0] * tile - 2 + y, 0)
        write(hid, pl.ds(at, 2 * pitch), jnp.where(keep, active, 0.0))
    spare = jnp.zeros((8 * pitch, channels), f32)
    write(hid, pl.ds(2 * pitch * rows, 8 * pitch), spare)
    write(dec, pl.ds(2 * pitch * rows, 8 * pitch), spare)

    inner = 2 * (tile + 2)
    main = inner * tile
    edge = 40
    for i in range(2 * rows):
        for dx in range(3):
            piece = read(hid, pl.ds(pitch * i + dx, tile)).astype(bf16)
            for dy in range(3):
                j = i - 2 * dy
                if 0 <= j < inner:
                    tap = (3 * dy + dx) * channels
                    taps[tile * j : tile * (j + 1), tap : tap + channels] = piece
    for dy in range(3):
        for x in range(tile, tile + 4):
            piece = read(hid, pl.ds(2 * pitch * dy + x, edge, stride=pitch)).astype(bf16)
            for e in range(2):
                dx = x - tile - e
                if 0 <= dx < 3:
                    tap = (3 * dy + dx) * channels
                    taps[main + edge * e : main + edge * (e + 1), tap : tap + channels] = piece

    conv = jnp.dot(taps[...], residual_ref[...], preferred_element_type=f32)
    column = real(at_ref[1] * tile - 1 + lax.broadcasted_iota(jnp.int32, (tile, 1), 0), 1)
    for i in range(inner):
        value = conv[tile * i : tile * (i + 1)] + read(dec, pl.ds(pitch * (i + 2) + 1, tile))
        keep = column & real(at_ref[0] * tile - 1 + i // 2, 0)
        write(ref, pl.ds(pitch * i, tile), jnp.where(keep, value, 0.0).astype(bf16).astype(f32))
    line = real(at_ref[0] * tile - 1 + lax.broadcasted_iota(jnp.int32, (edge, 1), 0) // 2, 0)
    for e in range(2):
        value = conv[main + edge * e : main + edge * (e + 1)]
        value += read(dec, pl.ds(2 * pitch + tile + 1 + e, edge, stride=pitch))
        keep = line & real(at_ref[1] * tile - 1 + tile + e, 1)
        value = jnp.where(keep, value, 0.0).astype(bf16).astype(f32)
        write(ref, pl.ds(tile + e, edge, stride=pitch), value)

    def column_parts(i):
        left, here, right = (read(ref, pl.ds(pitch * i + d, tile)) for d in range(3))
        return left - here, here, right - here

    for image in range(2):
        before = column_parts(image)
        for y in range(tile + 1):
            after = column_parts(2 * (y + 1) + image)
            at = tile * (2 * y + image)
            for q in range(3):
                slope[q, at : at + tile] = (before[q] - after[q]).astype(bf16)
                if y < tile:
                    centre[q, at : at + tile] = after[q].astype(bf16)
            before = after

    total = 2 * tile * tile

    def product(p, q):
        source = centre[q] if p == 1 else slope[q, tile * p : tile * p + total]
        return jnp.dot(source, upscale_ref[3 * p + q], preferred_element_type=f32)

    middle = product(1, 1)
    stores = []
    shared = (middle + product(1, 0), middle + product(1, 2))
    for a in range(2):
        between = product(2 * a, 1)
        for b in range(2):
            value = shared[b] + between + product(2 * a, 2 * b)
            write(mix.at[a], pl.ds(b, total, stride=2), value)
        for y in range(tile):
            for image in range(2):
                at = 2 * tile * (2 * y + image)
                out_ref[a, image, y] = read(mix.at[a], pl.ds(at, 2 * tile)).astype(bf16)
        stores.append(pltpu.make_async_copy(out_ref.at[a], out_hbm.at[:, :, a], sems.at[a]))
        stores[a].start()
    for store in stores:
        store.wait()


def keep_kernel(source_hbm, out_ref, sems):
    parts = sems.shape[0]
    size = source_hbm.shape[0] // parts
    copies = []
    for n in range(parts):
        at = pl.ds(n * size, size)
        copies.append(pltpu.make_async_copy(source_hbm.at[at], out_ref.at[at], sems.at[n]))
        copies[n].start()
    for copy in copies:
        copy.wait()


def keep(value):
    return pl.pallas_call(
        keep_kernel,
        out_shape=pltpu.VMEM(value.shape, value.dtype),
        in_specs=[pl.BlockSpec(memory_space=pl.ANY)],
        out_specs=pl.BlockSpec(memory_space=pltpu.VMEM),
        scratch_shapes=[pltpu.SemaphoreType.DMA((4,))],
        compiler_params=pltpu.CompilerParams(vmem_limit_bytes=16 << 20),
        cost_estimate=pl.CostEstimate(flops=0, bytes_accessed=2 * value.size, transcendentals=0),
        name="keep",
    )(value)


def phases_kernel(w_hbm, out_ref, w_ref, sems):
    parts = sems.shape[0]
    size = w_hbm.shape[1] // parts
    copies = []
    for n in range(parts):
        at = pl.ds(n * size, size)
        copies.append(pltpu.make_async_copy(w_hbm.at[:, at], w_ref.at[:, at], sems.at[n]))
        copies[n].start()
    for n in range(parts):
        copies[n].wait()
        at = pl.ds(n * size, size)
        wide = [w_ref[t, at].astype(jnp.float32) for t in range(9)]
        down = [
            [wide[q], wide[q] + wide[3 + q] + wide[6 + q], -wide[6 + q]] for q in range(3)
        ]
        for p in range(3):
            left, middle, right = (down[q][p] for q in range(3))
            out_ref[3 * p, at] = left.astype(jnp.bfloat16)
            out_ref[3 * p + 1, at] = (left + middle + right).astype(jnp.bfloat16)
            out_ref[3 * p + 2, at] = right.astype(jnp.bfloat16)


def phases(upscale):
    deep, channels = upscale.shape[2:]
    shape = (9, deep, channels)
    return pl.pallas_call(
        phases_kernel,
        out_shape=pltpu.VMEM(shape, jnp.bfloat16),
        in_specs=[pl.BlockSpec(memory_space=pl.ANY)],
        out_specs=pl.BlockSpec(memory_space=pltpu.VMEM),
        scratch_shapes=[pltpu.VMEM(shape, jnp.bfloat16), pltpu.SemaphoreType.DMA((8,))],
        compiler_params=pltpu.CompilerParams(vmem_limit_bytes=32 << 20),
        cost_estimate=pl.CostEstimate(flops=10 * deep * channels, bytes_accessed=18 * deep * channels, transcendentals=0),
        name="phases",
    )(upscale.reshape(shape))


def decode(at, latent, entry, gain, residual, combined, tiles):
    images, tile = latent.shape[0], 16
    channels = entry.shape[-1]
    pitch = 24
    padded = jnp.pad(latent, ((0, 0), (0, 0), (0, 10), (0, 0))).astype(jnp.float32)
    padded = padded.transpose(1, 0, 2, 3).reshape(images * (tile + 6), 32, latent.shape[-1])
    rows = images * (tile + 4) + 8
    inner = images * (tile + 2)
    total = images * tile * tile
    f32, bf16 = jnp.float32, jnp.bfloat16
    vmem = pl.BlockSpec(memory_space=pltpu.VMEM)
    hbm = pl.BlockSpec(memory_space=pl.ANY)
    out = pl.pallas_call(
        functools.partial(decode_kernel, tiles),
        out_shape=jax.ShapeDtypeStruct((images, tile, 2, 2 * tile, channels), bf16),
        in_specs=[pl.BlockSpec(memory_space=pltpu.SMEM)] + [vmem] * 5,
        out_specs=hbm,
        scratch_shapes=[
            pltpu.VMEM((images * (tile + 6) * pitch, 3 * latent.shape[-1]), bf16),
            pltpu.VMEM((channels // LANES, rows * pitch, LANES), f32),
            pltpu.VMEM((channels // LANES, rows * pitch, LANES), f32),
            pltpu.VMEM((inner * tile + 80, 9 * channels), bf16),
            pltpu.VMEM((channels // LANES, (inner + 4) * pitch, LANES), f32),
            pltpu.VMEM((3, total, channels), bf16),
            pltpu.VMEM((3, total + images * tile, channels), bf16),
            pltpu.VMEM((2, channels // LANES, 2 * total, LANES), f32),
            pltpu.VMEM((2, images, tile, 2 * tile, channels), bf16),
            pltpu.SemaphoreType.DMA((2,)),
        ],
        compiler_params=pltpu.CompilerParams(vmem_limit_bytes=40 << 20),
        cost_estimate=pl.CostEstimate(flops=8 * 10**9, bytes_accessed=12 << 20, transcendentals=0),
        name="decode",
    )(
        at,
        padded,
        entry.reshape(3, 3 * entry.shape[2], channels),
        gain.reshape(1, channels),
        residual,
        combined,
    )
    return out.reshape(images, 2 * tile, 2 * tile, channels)


def local(
    queries,
    key_rows_per_head,
    value_rows_per_head,
    latent_projection_weight,
    entry_conv_weight,
    residual_norm_gain,
    residual_conv_weight,
    upscale_conv_weight,
):
    images, tile, _, width = queries.shape
    scale = 1.0 / (tile * lax.axis_size("row") * tile * lax.axis_size("col"))
    flat = (images, tile * tile, width)
    keys, values = key_rows_per_head.reshape(flat), value_rows_per_head.reshape(flat)
    core = (lax.axis_index("col") % 2).astype(jnp.int32)
    mine, other = image_sums(keys, values, core, scale)
    channels = residual_conv_weight.shape[-1]
    residual = residual_conv_weight.reshape(9 * channels, channels)
    pieces, residual, combined = gather_all(mine, other, residual, upscale_conv_weight)
    row, col = lax.axis_index("row"), lax.axis_index("col")
    at = jnp.stack([row, col, row % 4]).astype(jnp.int32)
    latent = attend(at, queries.reshape(flat), pieces, latent_projection_weight)
    latent = latent.reshape(images, tile, tile, latent.shape[-1])
    widened = extended(latent, (("row", 1), ("col", 2)), 3)
    return decode(
        at,
        widened,
        entry_conv_weight,
        residual_norm_gain,
        residual,
        combined,
        (lax.axis_size("row"), lax.axis_size("col")),
    )


def solution(mesh):
    placed = (
        P(None, "row", "col", None),
        P(None, "row", "col", None),
        P(None, "row", "col", None),
        P(),
        P(),
        P(),
        P(),
        P(),
    )
    return jax.shard_map(
        local, mesh=mesh, in_specs=placed, out_specs=P(None, "row", "col", None), check_vma=False
    )
```

```python
import functools

import jax
import jax.numpy as jnp
from jax import lax
from jax.experimental import pallas as pl
from jax.experimental.pallas import tpu as pltpu
from jax.sharding import PartitionSpec as P

HEAD = 32
NORM_EPS = 1e-06
LANES = 128
PACK = 2560
KS_AT = 2304
WIDE = 3
SPLIT = (1, 3, 2)


def sums_kernel(scale, at_ref, k_hbm, v_hbm, mine_ref, other_ref, k_ref, v_ref, sems):
    images, tokens, width = k_ref.shape
    core = at_ref[3]
    half = tokens // 2
    copies = []
    for n in range(images):
        image = 1 - core if n == 0 else core
        for c in range(2):
            at = pl.ds(half * c, half)
            for m, (source, target) in enumerate(((k_hbm, k_ref), (v_hbm, v_ref))):
                copies.append(
                    pltpu.make_async_copy(source.at[image, at], target.at[n, at], sems.at[n, c, m])
                )
    for copy in copies:
        copy.start()
    ones = jnp.ones((tokens, LANES), jnp.bfloat16)
    lane = lax.broadcasted_iota(jnp.int32, (HEAD, LANES), 1)
    for n, out_ref in ((0, other_ref), (1, mine_ref)):
        for copy in copies[4 * n : 4 * n + 4]:
            copy.wait()
        parts = []
        key_sums = jnp.zeros((HEAD, LANES), jnp.float32)
        for start in range(0, width, LANES):
            size = min(LANES, width - start)
            keys = jnp.maximum(k_ref[n, :, start : start + size], 0)
            values = jnp.concatenate([v_ref[n, :, start : start + size], ones], axis=1)
            product = lax.dot_general(
                keys, values, (((0,), (0,)), ((), ())), preferred_element_type=jnp.float32
            )
            packed = jnp.zeros((HEAD, size), jnp.float32)
            for h in range(size // HEAD):
                rows = product[h * HEAD : (h + 1) * HEAD]
                packed = jnp.where(lane[:, :size] // HEAD == h, rows[:, :size], packed)
                key_sums = jnp.where(lane == start // HEAD + h, rows[:, size:], key_sums)
            parts.append(packed)
        parts.append(jnp.zeros((HEAD, KS_AT - width), jnp.float32))
        parts.append(key_sums)
        parts.append(jnp.zeros((HEAD, PACK - KS_AT - LANES), jnp.float32))
        total = (jnp.concatenate(parts, axis=1) * scale).astype(jnp.bfloat16)
        wide = PACK // 2
        for r in range(2):
            for c in range(2):
                out_ref[2 * r + c] = total[16 * r : 16 * r + 16, wide * c : wide * (c + 1)]


def image_sums(keys, values, at, scale):
    images, tokens, width = keys.shape
    out = pltpu.VMEM((4, 16, PACK // 2), jnp.bfloat16)
    vmem = pl.BlockSpec(memory_space=pltpu.VMEM)
    hbm = pl.BlockSpec(memory_space=pl.ANY)
    return pl.pallas_call(
        functools.partial(sums_kernel, scale),
        out_shape=[out, out],
        in_specs=[pl.BlockSpec(memory_space=pltpu.SMEM), hbm, hbm],
        out_specs=[vmem, vmem],
        scratch_shapes=[
            pltpu.VMEM(keys.shape, keys.dtype),
            pltpu.VMEM(values.shape, values.dtype),
            pltpu.SemaphoreType.DMA((images, 2, 2)),
        ],
        compiler_params=pltpu.CompilerParams(vmem_limit_bytes=56 << 20),
        cost_estimate=pl.CostEstimate(flops=4 * tokens * width * 256, bytes_accessed=8 * tokens * width, transcendentals=0),
        name="image_sums",
    )(at, keys, values)


def sides_kernel(q_ref, left_ref, right_ref):
    tokens = q_ref.shape[1]
    edge = left_ref.shape[1]
    side = 16
    row = lax.broadcasted_iota(jnp.int32, (2 * edge, tokens), 0)
    column = lax.broadcasted_iota(jnp.int32, (2 * edge, tokens), 1)
    place = row % edge
    wanted = side * (place // WIDE) + place % WIDE + (row // edge) * (side - WIDE)
    pick = (column == wanted).astype(jnp.bfloat16)
    picked = jnp.dot(pick, q_ref[0], preferred_element_type=jnp.float32).astype(jnp.bfloat16)
    left_ref[0] = picked[:edge]
    right_ref[0] = picked[edge:]


def sides(queries):
    images, tokens, width = queries.shape
    edge = 16 * WIDE
    out = jax.ShapeDtypeStruct((images, edge, width), queries.dtype)
    block = pl.BlockSpec((1, edge, width), lambda i: (i, 0, 0))
    return pl.pallas_call(
        sides_kernel,
        out_shape=[out, out],
        grid=(images,),
        in_specs=[pl.BlockSpec((1, tokens, width), lambda i: (i, 0, 0))],
        out_specs=[block, block],
        compiler_params=pltpu.CompilerParams(vmem_limit_bytes=48 << 20),
        cost_estimate=pl.CostEstimate(flops=10**9, bytes_accessed=3 * images * tokens * width, transcendentals=0),
        name="sides",
    )(queries)


def attend_kernel(
    at_ref, q_ref, left_ref, right_ref, piece0_ref, piece1_ref, piece2_ref, piece3_ref, weight_ref,
    out_ref, first_ref, last_ref, sums,
):
    f32, bf16 = jnp.float32, jnp.bfloat16
    images, inner, width = q_ref.shape
    edge = left_ref.shape[1]
    tokens = inner + 2 * edge
    tile = 16
    group = 2 * LANES
    for n, piece in enumerate((piece0_ref, piece1_ref, piece2_ref, piece3_ref)):
        sums[at_ref[2] ^ n] = piece[...]
    same = (
        lax.broadcasted_iota(jnp.int32, (group, group), 0) // HEAD
        == lax.broadcasted_iota(jnp.int32, (group, group), 1) // HEAD
    )
    same = same.astype(f32).astype(bf16)
    head_of = lax.broadcasted_iota(jnp.int32, (LANES, PACK), 0)
    lane_head = lax.broadcasted_iota(jnp.int32, (LANES, PACK), 1) // HEAD
    spread = (head_of == lane_head).astype(f32).astype(bf16)
    kv = [
        jnp.concatenate(
            [jnp.concatenate([sums[2 * r + c, image] for c in range(2)], axis=1) for r in range(2)], axis=0
        )
        for image in range(images)
    ]
    key_means = jnp.concatenate([part[:, KS_AT : KS_AT + LANES] for part in kv], axis=0)
    means = jnp.dot(key_means, spread, preferred_element_type=f32).astype(bf16)
    squares = [jnp.zeros((tokens, LANES), f32)] * images
    latent = jnp.zeros((images * tokens, weight_ref.shape[0]), f32)
    for start in range(0, width, group):
        size = min(group, width - start)
        repeat = size // HEAD
        here = same[:size, :size]
        parts = []
        for image in range(images):
            upper = kv[image][:, start : start + size]
            lower = means[HEAD * image : HEAD * (image + 1), start : start + size]
            lanes = slice(start, start + size)
            query = [ref[image, :, lanes] for ref in (q_ref, left_ref, right_ref)]
            query = jnp.maximum(jnp.concatenate(query, axis=0), 0)
            numerator = jnp.dot(
                query, jnp.concatenate([upper] * repeat, axis=0) * here, preferred_element_type=f32
            )
            denominator = jnp.dot(
                query, jnp.concatenate([lower] * repeat, axis=0) * here, preferred_element_type=f32
            )
            attended = numerator * pl.reciprocal(jnp.maximum(denominator, 1.0), approx=True)
            square = attended * attended
            for c in range(0, size, LANES):
                part = square[:, c : min(c + LANES, size)]
                if part.shape[1] < LANES:
                    rest = jnp.zeros((tokens, LANES - part.shape[1]), f32)
                    part = jnp.concatenate([part, rest], axis=1)
                squares[image] += part
            parts.append(attended.astype(bf16))
        latent += lax.dot_general(
            jnp.concatenate(parts, axis=0),
            weight_ref[:, start : start + size],
            (((1,), (1,)), ((), ())),
            preferred_element_type=f32,
        )
    for image in range(images):
        total = jnp.sum(squares[image], axis=1, keepdims=True)
        normed = latent[tokens * image : tokens * (image + 1)] * lax.rsqrt(total / width + NORM_EPS)
        normed = normed.astype(bf16).astype(f32)
        for y in range(tile):
            line = images * y + image
            at = inner + WIDE * y
            out_ref[line, :WIDE] = normed[at : at + WIDE]
            out_ref[line, WIDE : WIDE + tile] = normed[tile * y : tile * (y + 1)]
            at += edge
            out_ref[line, WIDE + tile : 2 * WIDE + tile] = normed[at : at + WIDE]
    out_ref[:, 2 * WIDE + tile :] = jnp.zeros((images * tile, 10, weight_ref.shape[0]), f32)
    first_ref[...] = out_ref[: images * WIDE]
    last_ref[...] = out_ref[images * (tile - WIDE) :]


def attend(at, queries, sides, pieces, weight):
    images, tokens, width = queries.shape
    channels = weight.shape[1]
    vmem = pl.BlockSpec(memory_space=pltpu.VMEM)
    return pl.pallas_call(
        attend_kernel,
        out_shape=[
            jax.ShapeDtypeStruct((images * lines, 32, channels), jnp.float32) for lines in (16, WIDE, WIDE)
        ],
        in_specs=[pl.BlockSpec(memory_space=pltpu.SMEM)] + [vmem] * 8,
        out_specs=[vmem] * 3,
        scratch_shapes=[pltpu.VMEM((4, images, 16, PACK // 2), jnp.bfloat16)],
        compiler_params=pltpu.CompilerParams(vmem_limit_bytes=32 << 20),
        cost_estimate=pl.CostEstimate(flops=2 * images * tokens * width * 512, bytes_accessed=2 * images * tokens * width, transcendentals=0),
        name="attend",
    )(at, queries, *sides, *pieces, weight.T)


def xor_pairs(distance):
    return [(i, i ^ distance) for i in range(16)]


def added(value, arrived):
    total = value.astype(jnp.float32)
    for part in arrived:
        total = total + part.astype(jnp.float32)
    return total.astype(jnp.bfloat16)


def sent(value, axis, distances):
    return [lax.ppermute(value, axis, xor_pairs(d)) for d in distances]


def shifted(first, last, axis):
    up = [(i, i + 1) for i in range(lax.axis_size(axis) - 1)]
    down = [(j, i) for i, j in up]
    return lax.ppermute(last, axis, up), lax.ppermute(first, axis, down)


def split_kernel(at_ref, mine_ref, arrived_ref, own_ref, *parts_ref):
    f32 = jnp.float32
    for d, out_ref in zip((0,) + SPLIT, (own_ref,) + parts_ref):
        chunk = at_ref[2] ^ d
        total = mine_ref[chunk].astype(f32) + arrived_ref[chunk].astype(f32)
        out_ref[...] = total.astype(out_ref.dtype)


def split(at, mine, arrived):
    shape = mine.shape[1:]
    vmem = pl.BlockSpec(memory_space=pltpu.VMEM)
    return pl.pallas_call(
        split_kernel,
        out_shape=[jax.ShapeDtypeStruct(shape, jnp.float32)]
        + [jax.ShapeDtypeStruct(shape, jnp.bfloat16)] * len(SPLIT),
        in_specs=[pl.BlockSpec(memory_space=pltpu.SMEM), vmem, vmem],
        out_specs=[vmem] * (1 + len(SPLIT)),
        compiler_params=pltpu.CompilerParams(vmem_limit_bytes=8 << 20),
        name="split",
    )(at, mine, arrived)


def join_kernel(at_ref, mine_ref, twin_ref, out_ref):
    core = at_ref[3]
    out_ref[core] = mine_ref[...]
    out_ref[1 - core] = twin_ref[...]


def join(at, mine, twin):
    vmem = pl.BlockSpec(memory_space=pltpu.VMEM)
    return pl.pallas_call(
        join_kernel,
        out_shape=jax.ShapeDtypeStruct((2, *mine.shape), mine.dtype),
        in_specs=[pl.BlockSpec(memory_space=pltpu.SMEM), vmem, vmem],
        out_specs=vmem,
        compiler_params=pltpu.CompilerParams(vmem_limit_bytes=8 << 20),
        name="join",
    )(at, mine, twin)


def gather_all(at, mine, other, queries, residual, upscale):
    hold = lax.optimization_barrier
    arrived = lax.ppermute(other, "col", xor_pairs(1))
    near, mine = hold((queries, mine))
    start, end = sides(near)
    arrived, start, end = hold((arrived, start, end))
    own, *parts = split(at, mine, arrived)
    parts = [lax.ppermute(part, "row", xor_pairs(d)) for part, d in zip(parts, SPLIT)]
    chunk = added(own, parts)

    chunk, weights, start, end = hold((chunk, residual, start, end))
    arrived = sent(chunk, "row", (4, 12, 8))
    beside = shifted(start, end, "col")
    arrived, kept = hold((arrived, keep(weights)))
    chunk = added(chunk, arrived)

    chunk = added(chunk, sent(chunk, "col", (2,)))

    chunk, weights = hold((chunk, upscale))
    arrived = sent(chunk, "col", (4, 12, 10))
    arrived, combined = hold((arrived, phases(weights)))
    chunk = added(chunk, arrived)

    twin = lax.ppermute(chunk, "col", xor_pairs(1))
    both = join(at, chunk, twin)
    pieces = [both] + sent(both, "row", (1, 2, 3))
    return pieces, beside, kept, combined


def read(ref, at):
    return jnp.concatenate([ref[c, at, :] for c in range(ref.shape[0])], axis=1)


def write(ref, at, value):
    for c in range(ref.shape[0]):
        ref[c, at, :] = value[:, LANES * c : LANES * (c + 1)]


def decode_kernel(
    tiles, at_ref, above_ref, lat_ref, below_ref, entry_ref, gain_ref, residual_ref, upscale_ref, out_hbm,
    wide, dec, hid, taps, ref, centre, slope, mix, out_ref, sems,
):
    tile = 16
    channels = out_hbm.shape[-1]
    pitch = 24
    f32, bf16 = jnp.float32, jnp.bfloat16
    rows = tile + 4
    spot = lax.broadcasted_iota(jnp.int32, (2 * pitch, 1), 0) % pitch

    def real(at, axis):
        return (at >= 0) & (at < tile * tiles[axis])

    for i in range(2 * (tile + 6)):
        source, line = (above_ref, i) if i < 2 * WIDE else (lat_ref, i - 2 * WIDE)
        if i >= 2 * (tile + WIDE):
            source, line = below_ref, i - 2 * (tile + WIDE)
        block = [source[line, dx : dx + pitch, :] for dx in range(3)]
        wide[pitch * i : pitch * (i + 1)] = jnp.concatenate(block, axis=1).astype(bf16)

    across = real(at_ref[1] * tile - 2 + spot, 1)
    gain = gain_ref[...]
    for y in range(rows):
        at = 2 * pitch * y
        value = jnp.dot(wide[at : at + 2 * pitch], entry_ref[0], preferred_element_type=f32)
        for dy in (1, 2):
            start = at + 2 * pitch * dy
            value += jnp.dot(wide[start : start + 2 * pitch], entry_ref[dy], preferred_element_type=f32)
        value = value.astype(bf16).astype(f32)
        write(dec, pl.ds(at, 2 * pitch), value)
        mean = jnp.mean(value * value, axis=1, keepdims=True)
        scaled = value * lax.rsqrt(mean + NORM_EPS) * gain
        active = 0.5 * scaled * (1.0 + jnp.tanh(0.5 * scaled))
        keep = across & real(at_ref[0] * tile - 2 + y, 0)
        write(hid, pl.ds(at, 2 * pitch), jnp.where(keep, active, 0.0))
    spare = jnp.zeros((8 * pitch, channels), f32)
    write(hid, pl.ds(2 * pitch * rows, 8 * pitch), spare)
    write(dec, pl.ds(2 * pitch * rows, 8 * pitch), spare)

    inner = 2 * (tile + 2)
    main = inner * tile
    edge = 40
    for i in range(2 * rows):
        for dx in range(3):
            piece = read(hid, pl.ds(pitch * i + dx, tile)).astype(bf16)
            for dy in range(3):
                j = i - 2 * dy
                if 0 <= j < inner:
                    tap = (3 * dy + dx) * channels
                    taps[tile * j : tile * (j + 1), tap : tap + channels] = piece
    for dy in range(3):
        for x in range(tile, tile + 4):
            piece = read(hid, pl.ds(2 * pitch * dy + x, edge, stride=pitch)).astype(bf16)
            for e in range(2):
                dx = x - tile - e
                if 0 <= dx < 3:
                    tap = (3 * dy + dx) * channels
                    taps[main + edge * e : main + edge * (e + 1), tap : tap + channels] = piece

    conv = jnp.dot(taps[...], residual_ref[...], preferred_element_type=f32)
    column = real(at_ref[1] * tile - 1 + lax.broadcasted_iota(jnp.int32, (tile, 1), 0), 1)
    for i in range(inner):
        value = conv[tile * i : tile * (i + 1)] + read(dec, pl.ds(pitch * (i + 2) + 1, tile))
        keep = column & real(at_ref[0] * tile - 1 + i // 2, 0)
        write(ref, pl.ds(pitch * i, tile), jnp.where(keep, value, 0.0).astype(bf16).astype(f32))
    line = real(at_ref[0] * tile - 1 + lax.broadcasted_iota(jnp.int32, (edge, 1), 0) // 2, 0)
    for e in range(2):
        value = conv[main + edge * e : main + edge * (e + 1)]
        value += read(dec, pl.ds(2 * pitch + tile + 1 + e, edge, stride=pitch))
        keep = line & real(at_ref[1] * tile - 1 + tile + e, 1)
        value = jnp.where(keep, value, 0.0).astype(bf16).astype(f32)
        write(ref, pl.ds(tile + e, edge, stride=pitch), value)

    def column_parts(i):
        left, here, right = (read(ref, pl.ds(pitch * i + d, tile)) for d in range(3))
        return left - here, here, right - here

    for image in range(2):
        before = column_parts(image)
        for y in range(tile + 1):
            after = column_parts(2 * (y + 1) + image)
            at = tile * (2 * y + image)
            for q in range(3):
                slope[q, at : at + tile] = (before[q] - after[q]).astype(bf16)
                if y < tile:
                    centre[q, at : at + tile] = after[q].astype(bf16)
            before = after

    total = 2 * tile * tile

    def product(p, q):
        source = centre[q] if p == 1 else slope[q, tile * p : tile * p + total]
        return jnp.dot(source, upscale_ref[3 * p + q], preferred_element_type=f32)

    middle = product(1, 1)
    stores = []
    shared = (middle + product(1, 0), middle + product(1, 2))
    for a in range(2):
        between = product(2 * a, 1)
        for b in range(2):
            value = shared[b] + between + product(2 * a, 2 * b)
            write(mix.at[a], pl.ds(b, total, stride=2), value)
        for y in range(tile):
            for image in range(2):
                at = 2 * tile * (2 * y + image)
                out_ref[a, image, y] = read(mix.at[a], pl.ds(at, 2 * tile)).astype(bf16)
        stores.append(pltpu.make_async_copy(out_ref.at[a], out_hbm.at[:, :, a], sems.at[a]))
        stores[a].start()
    for store in stores:
        store.wait()


def keep_kernel(source_hbm, out_ref, sems):
    parts = sems.shape[0]
    size = source_hbm.shape[0] // parts
    copies = []
    for n in range(parts):
        at = pl.ds(n * size, size)
        copies.append(pltpu.make_async_copy(source_hbm.at[at], out_ref.at[at], sems.at[n]))
        copies[n].start()
    for copy in copies:
        copy.wait()


def keep(value):
    return pl.pallas_call(
        keep_kernel,
        out_shape=pltpu.VMEM(value.shape, value.dtype),
        in_specs=[pl.BlockSpec(memory_space=pl.ANY)],
        out_specs=pl.BlockSpec(memory_space=pltpu.VMEM),
        scratch_shapes=[pltpu.SemaphoreType.DMA((4,))],
        compiler_params=pltpu.CompilerParams(vmem_limit_bytes=16 << 20),
        cost_estimate=pl.CostEstimate(flops=0, bytes_accessed=2 * value.size, transcendentals=0),
        name="keep",
    )(value)


def phases_kernel(w_hbm, out_ref, w_ref, sems):
    parts = sems.shape[0]
    size = w_hbm.shape[1] // parts
    copies = []
    for n in range(parts):
        at = pl.ds(n * size, size)
        copies.append(pltpu.make_async_copy(w_hbm.at[:, at], w_ref.at[:, at], sems.at[n]))
        copies[n].start()
    for n in range(parts):
        copies[n].wait()
        at = pl.ds(n * size, size)
        wide = [w_ref[t, at].astype(jnp.float32) for t in range(9)]
        down = [
            [wide[q], wide[q] + wide[3 + q] + wide[6 + q], -wide[6 + q]] for q in range(3)
        ]
        for p in range(3):
            left, middle, right = (down[q][p] for q in range(3))
            out_ref[3 * p, at] = left.astype(jnp.bfloat16)
            out_ref[3 * p + 1, at] = (left + middle + right).astype(jnp.bfloat16)
            out_ref[3 * p + 2, at] = right.astype(jnp.bfloat16)


def phases(upscale):
    deep, channels = upscale.shape[2:]
    shape = (9, deep, channels)
    return pl.pallas_call(
        phases_kernel,
        out_shape=pltpu.VMEM(shape, jnp.bfloat16),
        in_specs=[pl.BlockSpec(memory_space=pl.ANY)],
        out_specs=pl.BlockSpec(memory_space=pltpu.VMEM),
        scratch_shapes=[pltpu.VMEM(shape, jnp.bfloat16), pltpu.SemaphoreType.DMA((8,))],
        compiler_params=pltpu.CompilerParams(vmem_limit_bytes=32 << 20),
        cost_estimate=pl.CostEstimate(flops=10 * deep * channels, bytes_accessed=18 * deep * channels, transcendentals=0),
        name="phases",
    )(upscale.reshape(shape))


def decode(at, latent, entry, gain, residual, combined, tiles):
    images, tile = 2, 16
    latents = latent[1].shape[-1]
    channels = entry.shape[-1]
    pitch = 24
    rows = images * (tile + 4) + 8
    inner = images * (tile + 2)
    total = images * tile * tile
    f32, bf16 = jnp.float32, jnp.bfloat16
    vmem = pl.BlockSpec(memory_space=pltpu.VMEM)
    hbm = pl.BlockSpec(memory_space=pl.ANY)
    out = pl.pallas_call(
        functools.partial(decode_kernel, tiles),
        out_shape=jax.ShapeDtypeStruct((images, tile, 2, 2 * tile, channels), bf16),
        in_specs=[pl.BlockSpec(memory_space=pltpu.SMEM)] + [vmem] * 7,
        out_specs=hbm,
        scratch_shapes=[
            pltpu.VMEM((images * (tile + 6) * pitch, 3 * latents), bf16),
            pltpu.VMEM((channels // LANES, rows * pitch, LANES), f32),
            pltpu.VMEM((channels // LANES, rows * pitch, LANES), f32),
            pltpu.VMEM((inner * tile + 80, 9 * channels), bf16),
            pltpu.VMEM((channels // LANES, (inner + 4) * pitch, LANES), f32),
            pltpu.VMEM((3, total, channels), bf16),
            pltpu.VMEM((3, total + images * tile, channels), bf16),
            pltpu.VMEM((2, channels // LANES, 2 * total, LANES), f32),
            pltpu.VMEM((2, images, tile, 2 * tile, channels), bf16),
            pltpu.SemaphoreType.DMA((2,)),
        ],
        compiler_params=pltpu.CompilerParams(vmem_limit_bytes=40 << 20),
        cost_estimate=pl.CostEstimate(flops=8 * 10**9, bytes_accessed=12 << 20, transcendentals=0),
        name="decode",
    )(
        at,
        *latent,
        entry.reshape(3, 3 * entry.shape[2], channels),
        gain.reshape(1, channels),
        residual,
        combined,
    )
    return out.reshape(images, 2 * tile, 2 * tile, channels)


def local(
    queries,
    key_rows_per_head,
    value_rows_per_head,
    latent_projection_weight,
    entry_conv_weight,
    residual_norm_gain,
    residual_conv_weight,
    upscale_conv_weight,
):
    images, tile, _, width = queries.shape
    scale = 1.0 / (tile * lax.axis_size("row") * tile * lax.axis_size("col"))
    flat = (images, tile * tile, width)
    keys, values = key_rows_per_head.reshape(flat), value_rows_per_head.reshape(flat)
    row, col = lax.axis_index("row"), lax.axis_index("col")
    at = jnp.stack([row, col, row % 4, col % 2]).astype(jnp.int32)
    mine, other = image_sums(keys, values, at, scale)
    channels = residual_conv_weight.shape[-1]
    residual = residual_conv_weight.reshape(9 * channels, channels)
    queries = queries.reshape(flat)
    pieces, beside, residual, combined = gather_all(
        at, mine, other, queries, residual, upscale_conv_weight
    )
    latent, first, last = attend(at, queries, beside, pieces, latent_projection_weight)
    above, below = shifted(first, last, "row")
    return decode(
        at,
        (above, latent, below),
        entry_conv_weight,
        residual_norm_gain,
        residual,
        combined,
        (lax.axis_size("row"), lax.axis_size("col")),
    )


def solution(mesh):
    placed = (
        P(None, "row", "col", None),
        P(None, "row", "col", None),
        P(None, "row", "col", None),
        P(),
        P(),
        P(),
        P(),
        P(),
    )
    return jax.shard_map(
        local, mesh=mesh, in_specs=placed, out_specs=P(None, "row", "col", None), check_vma=False
    )
```

```python
import functools

import jax
import jax.numpy as jnp
from jax import lax
from jax.experimental import pallas as pl
from jax.experimental.pallas import tpu as pltpu
from jax.sharding import PartitionSpec as P

HEAD = 32
NORM_EPS = 1e-06
LANES = 128
PACK = 2560
KS_AT = 2304
WIDE = 3
SPLIT = (1, 3, 2)


def sums_kernel(scale, at_ref, k_hbm, v_hbm, mine_ref, other_ref, k_ref, v_ref, sems):
    images, tokens, width = k_ref.shape
    core = at_ref[3]
    half = tokens // 2
    copies = []
    for n in range(images):
        image = 1 - core if n == 0 else core
        for c in range(2):
            at = pl.ds(half * c, half)
            for m, (source, target) in enumerate(((k_hbm, k_ref), (v_hbm, v_ref))):
                copies.append(
                    pltpu.make_async_copy(source.at[image, at], target.at[n, at], sems.at[n, c, m])
                )
    for copy in copies:
        copy.start()
    ones = jnp.ones((tokens, LANES), jnp.bfloat16)
    lane = lax.broadcasted_iota(jnp.int32, (HEAD, LANES), 1)
    for n, out_ref in ((0, other_ref), (1, mine_ref)):
        for copy in copies[4 * n : 4 * n + 4]:
            copy.wait()
        parts = []
        key_sums = jnp.zeros((HEAD, LANES), jnp.float32)
        for start in range(0, width, LANES):
            size = min(LANES, width - start)
            keys = jnp.maximum(k_ref[n, :, start : start + size], 0)
            values = jnp.concatenate([v_ref[n, :, start : start + size], ones], axis=1)
            product = lax.dot_general(
                keys, values, (((0,), (0,)), ((), ())), preferred_element_type=jnp.float32
            )
            packed = jnp.zeros((HEAD, size), jnp.float32)
            for h in range(size // HEAD):
                rows = product[h * HEAD : (h + 1) * HEAD]
                packed = jnp.where(lane[:, :size] // HEAD == h, rows[:, :size], packed)
                key_sums = jnp.where(lane == start // HEAD + h, rows[:, size:], key_sums)
            parts.append(packed)
        parts.append(jnp.zeros((HEAD, KS_AT - width), jnp.float32))
        parts.append(key_sums)
        parts.append(jnp.zeros((HEAD, PACK - KS_AT - LANES), jnp.float32))
        total = (jnp.concatenate(parts, axis=1) * scale).astype(jnp.bfloat16)
        wide = PACK // 2
        for r in range(2):
            for c in range(2):
                out_ref[2 * r + c] = total[16 * r : 16 * r + 16, wide * c : wide * (c + 1)]


def image_sums(keys, values, at, scale):
    images, tokens, width = keys.shape
    out = pltpu.VMEM((4, 16, PACK // 2), jnp.bfloat16)
    vmem = pl.BlockSpec(memory_space=pltpu.VMEM)
    hbm = pl.BlockSpec(memory_space=pl.ANY)
    return pl.pallas_call(
        functools.partial(sums_kernel, scale),
        out_shape=[out, out],
        in_specs=[pl.BlockSpec(memory_space=pltpu.SMEM), hbm, hbm],
        out_specs=[vmem, vmem],
        scratch_shapes=[
            pltpu.VMEM(keys.shape, keys.dtype),
            pltpu.VMEM(values.shape, values.dtype),
            pltpu.SemaphoreType.DMA((images, 2, 2)),
        ],
        compiler_params=pltpu.CompilerParams(vmem_limit_bytes=56 << 20),
        cost_estimate=pl.CostEstimate(flops=4 * tokens * width * 256, bytes_accessed=8 * tokens * width, transcendentals=0),
        name="image_sums",
    )(at, keys, values)


def sides_kernel(at_ref, q_ref, near_ref, far_ref):
    tokens = q_ref.shape[1]
    edge = near_ref.shape[1]
    odd = at_ref[3] == 1
    side = 16
    row = lax.broadcasted_iota(jnp.int32, (2 * edge, tokens), 0)
    column = lax.broadcasted_iota(jnp.int32, (2 * edge, tokens), 1)
    place = row % edge
    wanted = side * (place // WIDE) + place % WIDE + (row // edge) * (side - WIDE)
    pick = (column == wanted).astype(jnp.bfloat16)
    picked = jnp.dot(pick, q_ref[0], preferred_element_type=jnp.float32).astype(jnp.bfloat16)
    near_ref[0] = jnp.where(odd, picked[:edge], picked[edge:])
    far_ref[0] = jnp.where(odd, picked[edge:], picked[:edge])


def sides(at, queries):
    images, tokens, width = queries.shape
    edge = 16 * WIDE
    out = jax.ShapeDtypeStruct((images, edge, width), queries.dtype)
    block = pl.BlockSpec((1, edge, width), lambda i: (i, 0, 0))
    return pl.pallas_call(
        sides_kernel,
        out_shape=[out, out],
        grid=(images,),
        in_specs=[
            pl.BlockSpec(memory_space=pltpu.SMEM),
            pl.BlockSpec((1, tokens, width), lambda i: (i, 0, 0)),
        ],
        out_specs=[block, block],
        compiler_params=pltpu.CompilerParams(vmem_limit_bytes=48 << 20),
        cost_estimate=pl.CostEstimate(flops=10**9, bytes_accessed=3 * images * tokens * width, transcendentals=0),
        name="sides",
    )(at, queries)


def attend_kernel(
    at_ref, q_ref, near_ref, far_ref, *rest,
):
    pieces, (weight_ref, out_ref, near_out_ref, far_out_ref, sums) = rest[:8], rest[8:]
    f32, bf16 = jnp.float32, jnp.bfloat16
    images, inner, width = q_ref.shape
    edge = near_ref.shape[1]
    odd = at_ref[3] == 1
    odd_row = at_ref[4] == 1
    tokens = inner + 2 * edge
    tile = 16
    group = 2 * LANES
    for n in range(4):
        sums[at_ref[2] ^ n, at_ref[3]] = pieces[n][...]
        sums[at_ref[2] ^ n, 1 - at_ref[3]] = pieces[4 + n][...]
    same = (
        lax.broadcasted_iota(jnp.int32, (group, group), 0) // HEAD
        == lax.broadcasted_iota(jnp.int32, (group, group), 1) // HEAD
    )
    same = same.astype(f32).astype(bf16)
    head_of = lax.broadcasted_iota(jnp.int32, (LANES, PACK), 0)
    lane_head = lax.broadcasted_iota(jnp.int32, (LANES, PACK), 1) // HEAD
    spread = (head_of == lane_head).astype(f32).astype(bf16)
    kv = [
        jnp.concatenate(
            [jnp.concatenate([sums[2 * r + c, image] for c in range(2)], axis=1) for r in range(2)], axis=0
        )
        for image in range(images)
    ]
    key_means = jnp.concatenate([part[:, KS_AT : KS_AT + LANES] for part in kv], axis=0)
    means = jnp.dot(key_means, spread, preferred_element_type=f32).astype(bf16)
    squares = [jnp.zeros((tokens, LANES), f32)] * images
    latent = jnp.zeros((images * tokens, weight_ref.shape[0]), f32)
    for start in range(0, width, group):
        size = min(group, width - start)
        repeat = size // HEAD
        here = same[:size, :size]
        parts = []
        for image in range(images):
            upper = kv[image][:, start : start + size]
            lower = means[HEAD * image : HEAD * (image + 1), start : start + size]
            lanes = slice(start, start + size)
            near, far = near_ref[image, :, lanes], far_ref[image, :, lanes]
            query = [q_ref[image, :, lanes], jnp.where(odd, near, far), jnp.where(odd, far, near)]
            query = jnp.maximum(jnp.concatenate(query, axis=0), 0)
            numerator = jnp.dot(
                query, jnp.concatenate([upper] * repeat, axis=0) * here, preferred_element_type=f32
            )
            denominator = jnp.dot(
                query, jnp.concatenate([lower] * repeat, axis=0) * here, preferred_element_type=f32
            )
            attended = numerator * pl.reciprocal(jnp.maximum(denominator, 1.0), approx=True)
            square = attended * attended
            for c in range(0, size, LANES):
                part = square[:, c : min(c + LANES, size)]
                if part.shape[1] < LANES:
                    rest = jnp.zeros((tokens, LANES - part.shape[1]), f32)
                    part = jnp.concatenate([part, rest], axis=1)
                squares[image] += part
            parts.append(attended.astype(bf16))
        latent += lax.dot_general(
            jnp.concatenate(parts, axis=0),
            weight_ref[:, start : start + size],
            (((1,), (1,)), ((), ())),
            preferred_element_type=f32,
        )
    for image in range(images):
        total = jnp.sum(squares[image], axis=1, keepdims=True)
        normed = latent[tokens * image : tokens * (image + 1)] * lax.rsqrt(total / width + NORM_EPS)
        normed = normed.astype(bf16).astype(f32)
        for y in range(tile):
            line = images * y + image
            at = inner + WIDE * y
            out_ref[line, :WIDE] = normed[at : at + WIDE]
            out_ref[line, WIDE : WIDE + tile] = normed[tile * y : tile * (y + 1)]
            at += edge
            out_ref[line, WIDE + tile : 2 * WIDE + tile] = normed[at : at + WIDE]
    out_ref[:, 2 * WIDE + tile :] = jnp.zeros((images * tile, 10, weight_ref.shape[0]), f32)
    first = out_ref[: images * WIDE]
    last = out_ref[images * (tile - WIDE) :]
    near_out_ref[...] = jnp.where(odd_row, first, last)
    far_out_ref[...] = jnp.where(odd_row, last, first)


def attend(at, queries, sides, pieces, weight):
    images, tokens, width = queries.shape
    channels = weight.shape[1]
    vmem = pl.BlockSpec(memory_space=pltpu.VMEM)
    return pl.pallas_call(
        attend_kernel,
        out_shape=[
            jax.ShapeDtypeStruct((images * lines, 32, channels), jnp.float32) for lines in (16, WIDE, WIDE)
        ],
        in_specs=[pl.BlockSpec(memory_space=pltpu.SMEM)] + [vmem] * 12,
        out_specs=[vmem] * 3,
        scratch_shapes=[pltpu.VMEM((4, images, 16, PACK // 2), jnp.bfloat16)],
        compiler_params=pltpu.CompilerParams(vmem_limit_bytes=32 << 20),
        cost_estimate=pl.CostEstimate(flops=2 * images * tokens * width * 512, bytes_accessed=2 * images * tokens * width, transcendentals=0),
        name="attend",
    )(at, queries, *sides, *pieces, weight.T)


def xor_pairs(distance):
    return [(i, i ^ distance) for i in range(16)]


def added(value, arrived):
    total = value.astype(jnp.float32)
    for part in arrived:
        total = total + part.astype(jnp.float32)
    return total.astype(jnp.bfloat16)


def sent(value, axis, distances):
    return [lax.ppermute(value, axis, xor_pairs(d)) for d in distances]


def swapped(even, odd, axis):
    size = lax.axis_size(axis)
    near = [(i, i ^ 1) for i in range(size)]
    far = [(i, i - 1 if i % 2 == 0 else i + 1) for i in range(1, size - 1)]
    return lax.ppermute(even, axis, near), lax.ppermute(odd, axis, far)


def split_kernel(at_ref, mine_ref, arrived_ref, own_ref, *parts_ref):
    f32 = jnp.float32
    for d, out_ref in zip((0,) + SPLIT, (own_ref,) + parts_ref):
        chunk = at_ref[2] ^ d
        total = mine_ref[chunk].astype(f32) + arrived_ref[chunk].astype(f32)
        out_ref[...] = total.astype(out_ref.dtype)


def split(at, mine, arrived):
    shape = mine.shape[1:]
    vmem = pl.BlockSpec(memory_space=pltpu.VMEM)
    return pl.pallas_call(
        split_kernel,
        out_shape=[jax.ShapeDtypeStruct(shape, jnp.float32)]
        + [jax.ShapeDtypeStruct(shape, jnp.bfloat16)] * len(SPLIT),
        in_specs=[pl.BlockSpec(memory_space=pltpu.SMEM), vmem, vmem],
        out_specs=[vmem] * (1 + len(SPLIT)),
        compiler_params=pltpu.CompilerParams(vmem_limit_bytes=8 << 20),
        name="split",
    )(at, mine, arrived)


def gather_all(at, mine, other, queries, residual, upscale):
    hold = lax.optimization_barrier
    arrived = lax.ppermute(other, "col", xor_pairs(1))
    near, mine = hold((queries, mine))
    start, end = sides(at, near)
    arrived, start, end = hold((arrived, start, end))
    own, *parts = split(at, mine, arrived)
    parts = [lax.ppermute(part, "row", xor_pairs(d)) for part, d in zip(parts, SPLIT)]
    chunk = added(own, parts)

    chunk, weights, start, end = hold((chunk, residual, start, end))
    arrived = sent(chunk, "row", (4, 12, 8))
    beside = swapped(start, end, "col")
    arrived, kept = hold((arrived, keep(weights)))
    chunk = added(chunk, arrived)

    chunk = added(chunk, sent(chunk, "col", (2,)))

    chunk, weights = hold((chunk, upscale))
    arrived = sent(chunk, "col", (4, 12, 10))
    arrived, combined = hold((arrived, phases(weights)))
    chunk = added(chunk, arrived)

    pieces = [chunk] + sent(chunk, "row", (1, 2, 3))
    pieces += [lax.ppermute(piece, "col", xor_pairs(1)) for piece in pieces]
    return pieces, beside, kept, combined


def read(ref, at):
    return jnp.concatenate([ref[c, at, :] for c in range(ref.shape[0])], axis=1)


def write(ref, at, value):
    for c in range(ref.shape[0]):
        ref[c, at, :] = value[:, LANES * c : LANES * (c + 1)]


def decode_kernel(
    tiles, at_ref, lat_ref, near_ref, far_ref, entry_ref, gain_ref, residual_ref, upscale_ref, out_hbm,
    wide, dec, hid, taps, ref, centre, slope, mix, out_ref, sems,
):
    tile = 16
    channels = out_hbm.shape[-1]
    pitch = 24
    f32, bf16 = jnp.float32, jnp.bfloat16
    rows = tile + 4
    odd = at_ref[4] == 1
    spot = lax.broadcasted_iota(jnp.int32, (2 * pitch, 1), 0) % pitch

    def real(at, axis):
        return (at >= 0) & (at < tile * tiles[axis])

    for i in range(2 * (tile + 6)):
        if i < 2 * WIDE:
            line = jnp.where(odd, near_ref[i], far_ref[i])
        elif i < 2 * (tile + WIDE):
            line = lat_ref[i - 2 * WIDE]
        else:
            line = i - 2 * (tile + WIDE)
            line = jnp.where(odd, far_ref[line], near_ref[line])
        block = [line[dx : dx + pitch] for dx in range(3)]
        wide[pitch * i : pitch * (i + 1)] = jnp.concatenate(block, axis=1).astype(bf16)

    across = real(at_ref[1] * tile - 2 + spot, 1)
    gain = gain_ref[...]
    for y in range(rows):
        at = 2 * pitch * y
        value = jnp.dot(wide[at : at + 2 * pitch], entry_ref[0], preferred_element_type=f32)
        for dy in (1, 2):
            start = at + 2 * pitch * dy
            value += jnp.dot(wide[start : start + 2 * pitch], entry_ref[dy], preferred_element_type=f32)
        value = value.astype(bf16).astype(f32)
        write(dec, pl.ds(at, 2 * pitch), value)
        mean = jnp.mean(value * value, axis=1, keepdims=True)
        scaled = value * lax.rsqrt(mean + NORM_EPS) * gain
        active = 0.5 * scaled * (1.0 + jnp.tanh(0.5 * scaled))
        keep = across & real(at_ref[0] * tile - 2 + y, 0)
        write(hid, pl.ds(at, 2 * pitch), jnp.where(keep, active, 0.0))
    spare = jnp.zeros((8 * pitch, channels), f32)
    write(hid, pl.ds(2 * pitch * rows, 8 * pitch), spare)
    write(dec, pl.ds(2 * pitch * rows, 8 * pitch), spare)

    inner = 2 * (tile + 2)
    main = inner * tile
    edge = 40
    for i in range(2 * rows):
        for dx in range(3):
            piece = read(hid, pl.ds(pitch * i + dx, tile)).astype(bf16)
            for dy in range(3):
                j = i - 2 * dy
                if 0 <= j < inner:
                    tap = (3 * dy + dx) * channels
                    taps[tile * j : tile * (j + 1), tap : tap + channels] = piece
    for dy in range(3):
        for x in range(tile, tile + 4):
            piece = read(hid, pl.ds(2 * pitch * dy + x, edge, stride=pitch)).astype(bf16)
            for e in range(2):
                dx = x - tile - e
                if 0 <= dx < 3:
                    tap = (3 * dy + dx) * channels
                    taps[main + edge * e : main + edge * (e + 1), tap : tap + channels] = piece

    conv = jnp.dot(taps[...], residual_ref[...], preferred_element_type=f32)
    column = real(at_ref[1] * tile - 1 + lax.broadcasted_iota(jnp.int32, (tile, 1), 0), 1)
    for i in range(inner):
        value = conv[tile * i : tile * (i + 1)] + read(dec, pl.ds(pitch * (i + 2) + 1, tile))
        keep = column & real(at_ref[0] * tile - 1 + i // 2, 0)
        write(ref, pl.ds(pitch * i, tile), jnp.where(keep, value, 0.0).astype(bf16).astype(f32))
    line = real(at_ref[0] * tile - 1 + lax.broadcasted_iota(jnp.int32, (edge, 1), 0) // 2, 0)
    for e in range(2):
        value = conv[main + edge * e : main + edge * (e + 1)]
        value += read(dec, pl.ds(2 * pitch + tile + 1 + e, edge, stride=pitch))
        keep = line & real(at_ref[1] * tile - 1 + tile + e, 1)
        value = jnp.where(keep, value, 0.0).astype(bf16).astype(f32)
        write(ref, pl.ds(tile + e, edge, stride=pitch), value)

    def column_parts(i):
        left, here, right = (read(ref, pl.ds(pitch * i + d, tile)) for d in range(3))
        return left - here, here, right - here

    for image in range(2):
        before = column_parts(image)
        for y in range(tile + 1):
            after = column_parts(2 * (y + 1) + image)
            at = tile * (2 * y + image)
            for q in range(3):
                slope[q, at : at + tile] = (before[q] - after[q]).astype(bf16)
                if y < tile:
                    centre[q, at : at + tile] = after[q].astype(bf16)
            before = after

    total = 2 * tile * tile

    def product(p, q):
        source = centre[q] if p == 1 else slope[q, tile * p : tile * p + total]
        return jnp.dot(source, upscale_ref[3 * p + q], preferred_element_type=f32)

    middle = product(1, 1)
    stores = []
    shared = (middle + product(1, 0), middle + product(1, 2))
    for a in range(2):
        between = product(2 * a, 1)
        for b in range(2):
            value = shared[b] + between + product(2 * a, 2 * b)
            write(mix.at[a], pl.ds(b, total, stride=2), value)
        for y in range(tile):
            for image in range(2):
                at = 2 * tile * (2 * y + image)
                out_ref[a, image, y] = read(mix.at[a], pl.ds(at, 2 * tile)).astype(bf16)
        stores.append(pltpu.make_async_copy(out_ref.at[a], out_hbm.at[:, :, a], sems.at[a]))
        stores[a].start()
    for store in stores:
        store.wait()


def keep_kernel(source_hbm, out_ref, sems):
    parts = sems.shape[0]
    size = source_hbm.shape[0] // parts
    copies = []
    for n in range(parts):
        at = pl.ds(n * size, size)
        copies.append(pltpu.make_async_copy(source_hbm.at[at], out_ref.at[at], sems.at[n]))
        copies[n].start()
    for copy in copies:
        copy.wait()


def keep(value):
    return pl.pallas_call(
        keep_kernel,
        out_shape=pltpu.VMEM(value.shape, value.dtype),
        in_specs=[pl.BlockSpec(memory_space=pl.ANY)],
        out_specs=pl.BlockSpec(memory_space=pltpu.VMEM),
        scratch_shapes=[pltpu.SemaphoreType.DMA((4,))],
        compiler_params=pltpu.CompilerParams(vmem_limit_bytes=16 << 20),
        cost_estimate=pl.CostEstimate(flops=0, bytes_accessed=2 * value.size, transcendentals=0),
        name="keep",
    )(value)


def phases_kernel(w_hbm, out_ref, w_ref, sems):
    parts = sems.shape[0]
    size = w_hbm.shape[1] // parts
    copies = []
    for n in range(parts):
        at = pl.ds(n * size, size)
        copies.append(pltpu.make_async_copy(w_hbm.at[:, at], w_ref.at[:, at], sems.at[n]))
        copies[n].start()
    for n in range(parts):
        copies[n].wait()
        at = pl.ds(n * size, size)
        wide = [w_ref[t, at].astype(jnp.float32) for t in range(9)]
        down = [
            [wide[q], wide[q] + wide[3 + q] + wide[6 + q], -wide[6 + q]] for q in range(3)
        ]
        for p in range(3):
            left, middle, right = (down[q][p] for q in range(3))
            out_ref[3 * p, at] = left.astype(jnp.bfloat16)
            out_ref[3 * p + 1, at] = (left + middle + right).astype(jnp.bfloat16)
            out_ref[3 * p + 2, at] = right.astype(jnp.bfloat16)


def phases(upscale):
    deep, channels = upscale.shape[2:]
    shape = (9, deep, channels)
    return pl.pallas_call(
        phases_kernel,
        out_shape=pltpu.VMEM(shape, jnp.bfloat16),
        in_specs=[pl.BlockSpec(memory_space=pl.ANY)],
        out_specs=pl.BlockSpec(memory_space=pltpu.VMEM),
        scratch_shapes=[pltpu.VMEM(shape, jnp.bfloat16), pltpu.SemaphoreType.DMA((8,))],
        compiler_params=pltpu.CompilerParams(vmem_limit_bytes=32 << 20),
        cost_estimate=pl.CostEstimate(flops=10 * deep * channels, bytes_accessed=18 * deep * channels, transcendentals=0),
        name="phases",
    )(upscale.reshape(shape))


def decode(at, latent, entry, gain, residual, combined, tiles):
    images, tile = 2, 16
    latents = latent[0].shape[-1]
    channels = entry.shape[-1]
    pitch = 24
    rows = images * (tile + 4) + 8
    inner = images * (tile + 2)
    total = images * tile * tile
    f32, bf16 = jnp.float32, jnp.bfloat16
    vmem = pl.BlockSpec(memory_space=pltpu.VMEM)
    hbm = pl.BlockSpec(memory_space=pl.ANY)
    out = pl.pallas_call(
        functools.partial(decode_kernel, tiles),
        out_shape=jax.ShapeDtypeStruct((images, tile, 2, 2 * tile, channels), bf16),
        in_specs=[pl.BlockSpec(memory_space=pltpu.SMEM)] + [vmem] * 7,
        out_specs=hbm,
        scratch_shapes=[
            pltpu.VMEM((images * (tile + 6) * pitch, 3 * latents), bf16),
            pltpu.VMEM((channels // LANES, rows * pitch, LANES), f32),
            pltpu.VMEM((channels // LANES, rows * pitch, LANES), f32),
            pltpu.VMEM((inner * tile + 80, 9 * channels), bf16),
            pltpu.VMEM((channels // LANES, (inner + 4) * pitch, LANES), f32),
            pltpu.VMEM((3, total, channels), bf16),
            pltpu.VMEM((3, total + images * tile, channels), bf16),
            pltpu.VMEM((2, channels // LANES, 2 * total, LANES), f32),
            pltpu.VMEM((2, images, tile, 2 * tile, channels), bf16),
            pltpu.SemaphoreType.DMA((2,)),
        ],
        compiler_params=pltpu.CompilerParams(vmem_limit_bytes=40 << 20),
        cost_estimate=pl.CostEstimate(flops=8 * 10**9, bytes_accessed=12 << 20, transcendentals=0),
        name="decode",
    )(
        at,
        *latent,
        entry.reshape(3, 3 * entry.shape[2], channels),
        gain.reshape(1, channels),
        residual,
        combined,
    )
    return out.reshape(images, 2 * tile, 2 * tile, channels)


def local(
    queries,
    key_rows_per_head,
    value_rows_per_head,
    latent_projection_weight,
    entry_conv_weight,
    residual_norm_gain,
    residual_conv_weight,
    upscale_conv_weight,
):
    images, tile, _, width = queries.shape
    scale = 1.0 / (tile * lax.axis_size("row") * tile * lax.axis_size("col"))
    flat = (images, tile * tile, width)
    keys, values = key_rows_per_head.reshape(flat), value_rows_per_head.reshape(flat)
    row, col = lax.axis_index("row"), lax.axis_index("col")
    at = jnp.stack([row, col, row % 4, col % 2, row % 2]).astype(jnp.int32)
    mine, other = image_sums(keys, values, at, scale)
    channels = residual_conv_weight.shape[-1]
    residual = residual_conv_weight.reshape(9 * channels, channels)
    queries = queries.reshape(flat)
    pieces, beside, residual, combined = gather_all(
        at, mine, other, queries, residual, upscale_conv_weight
    )
    latent, near, far = attend(at, queries, beside, pieces, latent_projection_weight)
    near, far = swapped(near, far, "row")
    return decode(
        at,
        (latent, near, far),
        entry_conv_weight,
        residual_norm_gain,
        residual,
        combined,
        (lax.axis_size("row"), lax.axis_size("col")),
    )


def solution(mesh):
    placed = (
        P(None, "row", "col", None),
        P(None, "row", "col", None),
        P(None, "row", "col", None),
        P(),
        P(),
        P(),
        P(),
        P(),
    )
    return jax.shard_map(
        local, mesh=mesh, in_specs=placed, out_specs=P(None, "row", "col", None), check_vma=False
    )
```

```python
import functools

import jax
import jax.numpy as jnp
from jax import lax
from jax.experimental import pallas as pl
from jax.experimental.pallas import tpu as pltpu
from jax.sharding import PartitionSpec as P

HEAD = 32
NORM_EPS = 1e-06
LANES = 128
PACK = 2560
KS_AT = 2304
WIDE = 3
SPLIT = (1, 3, 2)


def position():
    row, col = lax.axis_index("row"), lax.axis_index("col")
    return row, col, lax.rem(row, 4), lax.rem(col, 2), lax.rem(row, 2)


def sums_kernel(scale, k_hbm, v_hbm, mine_ref, other_ref, k_ref, v_ref, sems):
    images, tokens, width = k_ref.shape
    core = position()[3]
    half = tokens // 2
    copies = []
    for n in range(images):
        image = 1 - core if n == 0 else core
        for c in range(2):
            at = pl.ds(half * c, half)
            for m, (source, target) in enumerate(((k_hbm, k_ref), (v_hbm, v_ref))):
                copies.append(
                    pltpu.make_async_copy(source.at[image, at], target.at[n, at], sems.at[n, c, m])
                )
    for copy in copies:
        copy.start()
    ones = jnp.ones((tokens, LANES), jnp.bfloat16)
    lane = lax.broadcasted_iota(jnp.int32, (HEAD, LANES), 1)
    for n, out_ref in ((0, other_ref), (1, mine_ref)):
        for copy in copies[4 * n : 4 * n + 4]:
            copy.wait()
        parts = []
        key_sums = jnp.zeros((HEAD, LANES), jnp.float32)
        for start in range(0, width, LANES):
            size = min(LANES, width - start)
            keys = jnp.maximum(k_ref[n, :, start : start + size], 0)
            values = jnp.concatenate([v_ref[n, :, start : start + size], ones], axis=1)
            product = lax.dot_general(
                keys, values, (((0,), (0,)), ((), ())), preferred_element_type=jnp.float32
            )
            packed = jnp.zeros((HEAD, size), jnp.float32)
            for h in range(size // HEAD):
                rows = product[h * HEAD : (h + 1) * HEAD]
                packed = jnp.where(lane[:, :size] // HEAD == h, rows[:, :size], packed)
                key_sums = jnp.where(lane == start // HEAD + h, rows[:, size:], key_sums)
            parts.append(packed)
        parts.append(jnp.zeros((HEAD, KS_AT - width), jnp.float32))
        parts.append(key_sums)
        parts.append(jnp.zeros((HEAD, PACK - KS_AT - LANES), jnp.float32))
        total = (jnp.concatenate(parts, axis=1) * scale).astype(jnp.bfloat16)
        wide = PACK // 2
        for r in range(2):
            for c in range(2):
                out_ref[2 * r + c] = total[16 * r : 16 * r + 16, wide * c : wide * (c + 1)]


def image_sums(keys, values, scale):
    images, tokens, width = keys.shape
    out = pltpu.VMEM((4, 16, PACK // 2), jnp.bfloat16)
    vmem = pl.BlockSpec(memory_space=pltpu.VMEM)
    hbm = pl.BlockSpec(memory_space=pl.ANY)
    return pl.pallas_call(
        functools.partial(sums_kernel, scale),
        out_shape=[out, out],
        in_specs=[hbm, hbm],
        out_specs=[vmem, vmem],
        scratch_shapes=[
            pltpu.VMEM(keys.shape, keys.dtype),
            pltpu.VMEM(values.shape, values.dtype),
            pltpu.SemaphoreType.DMA((images, 2, 2)),
        ],
        compiler_params=pltpu.CompilerParams(vmem_limit_bytes=56 << 20),
        cost_estimate=pl.CostEstimate(flops=4 * tokens * width * 256, bytes_accessed=8 * tokens * width, transcendentals=0),
        name="image_sums",
    )(keys, values)


def sides_kernel(q_ref, near_ref, far_ref):
    at_ref = position()
    tokens = q_ref.shape[1]
    edge = near_ref.shape[1]
    odd = at_ref[3] == 1
    side = 16
    row = lax.broadcasted_iota(jnp.int32, (2 * edge, tokens), 0)
    column = lax.broadcasted_iota(jnp.int32, (2 * edge, tokens), 1)
    place = row % edge
    wanted = side * (place // WIDE) + place % WIDE + (row // edge) * (side - WIDE)
    pick = (column == wanted).astype(jnp.bfloat16)
    picked = jnp.dot(pick, q_ref[0], preferred_element_type=jnp.float32).astype(jnp.bfloat16)
    near_ref[0] = jnp.where(odd, picked[:edge], picked[edge:])
    far_ref[0] = jnp.where(odd, picked[edge:], picked[:edge])


def sides(queries):
    images, tokens, width = queries.shape
    edge = 16 * WIDE
    out = jax.ShapeDtypeStruct((images, edge, width), queries.dtype)
    block = pl.BlockSpec((1, edge, width), lambda i: (i, 0, 0))
    return pl.pallas_call(
        sides_kernel,
        out_shape=[out, out],
        grid=(images,),
        in_specs=[pl.BlockSpec((1, tokens, width), lambda i: (i, 0, 0))],
        out_specs=[block, block],
        compiler_params=pltpu.CompilerParams(vmem_limit_bytes=48 << 20),
        cost_estimate=pl.CostEstimate(flops=10**9, bytes_accessed=3 * images * tokens * width, transcendentals=0),
        name="sides",
    )(queries)


def attend_kernel(
    q_ref, near_ref, far_ref, *rest,
):
    at_ref = position()
    pieces, (weight_ref, out_ref, near_out_ref, far_out_ref, sums) = rest[:8], rest[8:]
    f32, bf16 = jnp.float32, jnp.bfloat16
    images, inner, width = q_ref.shape
    edge = near_ref.shape[1]
    odd = at_ref[3] == 1
    odd_row = at_ref[4] == 1
    tokens = inner + 2 * edge
    tile = 16
    group = 2 * LANES
    for n in range(4):
        sums[at_ref[2] ^ n, at_ref[3]] = pieces[n][...]
        sums[at_ref[2] ^ n, 1 - at_ref[3]] = pieces[4 + n][...]
    same = (
        lax.broadcasted_iota(jnp.int32, (group, group), 0) // HEAD
        == lax.broadcasted_iota(jnp.int32, (group, group), 1) // HEAD
    )
    same = same.astype(f32).astype(bf16)
    head_of = lax.broadcasted_iota(jnp.int32, (LANES, PACK), 0)
    lane_head = lax.broadcasted_iota(jnp.int32, (LANES, PACK), 1) // HEAD
    spread = (head_of == lane_head).astype(f32).astype(bf16)
    kv = [
        jnp.concatenate(
            [jnp.concatenate([sums[2 * r + c, image] for c in range(2)], axis=1) for r in range(2)], axis=0
        )
        for image in range(images)
    ]
    key_means = jnp.concatenate([part[:, KS_AT : KS_AT + LANES] for part in kv], axis=0)
    means = jnp.dot(key_means, spread, preferred_element_type=f32).astype(bf16)
    squares = [jnp.zeros((tokens, LANES), f32)] * images
    latent = jnp.zeros((images * tokens, weight_ref.shape[0]), f32)
    for start in range(0, width, group):
        size = min(group, width - start)
        repeat = size // HEAD
        here = same[:size, :size]
        parts = []
        for image in range(images):
            upper = kv[image][:, start : start + size]
            lower = means[HEAD * image : HEAD * (image + 1), start : start + size]
            lanes = slice(start, start + size)
            near, far = near_ref[image, :, lanes], far_ref[image, :, lanes]
            query = [q_ref[image, :, lanes], jnp.where(odd, near, far), jnp.where(odd, far, near)]
            query = jnp.maximum(jnp.concatenate(query, axis=0), 0)
            numerator = jnp.dot(
                query, jnp.concatenate([upper] * repeat, axis=0) * here, preferred_element_type=f32
            )
            denominator = jnp.dot(
                query, jnp.concatenate([lower] * repeat, axis=0) * here, preferred_element_type=f32
            )
            attended = numerator * pl.reciprocal(jnp.maximum(denominator, 1.0), approx=True)
            square = attended * attended
            for c in range(0, size, LANES):
                part = square[:, c : min(c + LANES, size)]
                if part.shape[1] < LANES:
                    rest = jnp.zeros((tokens, LANES - part.shape[1]), f32)
                    part = jnp.concatenate([part, rest], axis=1)
                squares[image] += part
            parts.append(attended.astype(bf16))
        latent += lax.dot_general(
            jnp.concatenate(parts, axis=0),
            weight_ref[:, start : start + size],
            (((1,), (1,)), ((), ())),
            preferred_element_type=f32,
        )
    for image in range(images):
        total = jnp.sum(squares[image], axis=1, keepdims=True)
        normed = latent[tokens * image : tokens * (image + 1)] * lax.rsqrt(total / width + NORM_EPS)
        normed = normed.astype(bf16).astype(f32)
        for y in range(tile):
            line = images * y + image
            at = inner + WIDE * y
            out_ref[line, :WIDE] = normed[at : at + WIDE]
            out_ref[line, WIDE : WIDE + tile] = normed[tile * y : tile * (y + 1)]
            at += edge
            out_ref[line, WIDE + tile : 2 * WIDE + tile] = normed[at : at + WIDE]
    out_ref[:, 2 * WIDE + tile :] = jnp.zeros((images * tile, 10, weight_ref.shape[0]), f32)
    first = out_ref[: images * WIDE]
    last = out_ref[images * (tile - WIDE) :]
    near_out_ref[...] = jnp.where(odd_row, first, last)
    far_out_ref[...] = jnp.where(odd_row, last, first)


def attend(queries, sides, pieces, weight):
    images, tokens, width = queries.shape
    channels = weight.shape[1]
    vmem = pl.BlockSpec(memory_space=pltpu.VMEM)
    return pl.pallas_call(
        attend_kernel,
        out_shape=[
            jax.ShapeDtypeStruct((images * lines, 32, channels), jnp.float32) for lines in (16, WIDE, WIDE)
        ],
        in_specs=[vmem] * 12,
        out_specs=[vmem] * 3,
        scratch_shapes=[pltpu.VMEM((4, images, 16, PACK // 2), jnp.bfloat16)],
        compiler_params=pltpu.CompilerParams(vmem_limit_bytes=32 << 20),
        cost_estimate=pl.CostEstimate(flops=2 * images * tokens * width * 512, bytes_accessed=2 * images * tokens * width, transcendentals=0),
        name="attend",
    )(queries, *sides, *pieces, weight.T)


def xor_pairs(distance):
    return [(i, i ^ distance) for i in range(16)]


def added(value, arrived):
    total = value.astype(jnp.float32)
    for part in arrived:
        total = total + part.astype(jnp.float32)
    return total.astype(jnp.bfloat16)


def sent(value, axis, distances):
    return [lax.ppermute(value, axis, xor_pairs(d)) for d in distances]


def swapped(even, odd, axis):
    size = lax.axis_size(axis)
    near = [(i, i ^ 1) for i in range(size)]
    far = [(i, i - 1 if i % 2 == 0 else i + 1) for i in range(1, size - 1)]
    return lax.ppermute(even, axis, near), lax.ppermute(odd, axis, far)


def split_kernel(mine_ref, arrived_ref, own_ref, *parts_ref):
    at_ref = position()
    f32 = jnp.float32
    for d, out_ref in zip((0,) + SPLIT, (own_ref,) + parts_ref):
        chunk = at_ref[2] ^ d
        total = mine_ref[chunk].astype(f32) + arrived_ref[chunk].astype(f32)
        out_ref[...] = total.astype(out_ref.dtype)


def split(mine, arrived):
    shape = mine.shape[1:]
    vmem = pl.BlockSpec(memory_space=pltpu.VMEM)
    return pl.pallas_call(
        split_kernel,
        out_shape=[jax.ShapeDtypeStruct(shape, jnp.float32)]
        + [jax.ShapeDtypeStruct(shape, jnp.bfloat16)] * len(SPLIT),
        in_specs=[vmem, vmem],
        out_specs=[vmem] * (1 + len(SPLIT)),
        compiler_params=pltpu.CompilerParams(vmem_limit_bytes=8 << 20),
        name="split",
    )(mine, arrived)


def gather_all(mine, other, queries, residual, upscale):
    hold = lax.optimization_barrier
    arrived = lax.ppermute(other, "col", xor_pairs(1))
    near, mine = hold((queries, mine))
    start, end = sides(near)
    arrived, start, end = hold((arrived, start, end))
    own, *parts = split(mine, arrived)
    parts = [lax.ppermute(part, "row", xor_pairs(d)) for part, d in zip(parts, SPLIT)]
    chunk = added(own, parts)

    chunk, weights, start, end = hold((chunk, residual, start, end))
    arrived = sent(chunk, "row", (4, 12, 8))
    beside = swapped(start, end, "col")
    arrived, kept = hold((arrived, keep(weights)))
    chunk = added(chunk, arrived)

    chunk = added(chunk, sent(chunk, "col", (2,)))

    chunk, weights = hold((chunk, upscale))
    arrived = sent(chunk, "col", (4, 12, 10))
    arrived, combined = hold((arrived, phases(weights)))
    chunk = added(chunk, arrived)

    pieces = [chunk] + sent(chunk, "row", (1, 2, 3))
    pieces += [lax.ppermute(piece, "col", xor_pairs(1)) for piece in pieces]
    return pieces, beside, kept, combined


def read(ref, at):
    return jnp.concatenate([ref[c, at, :] for c in range(ref.shape[0])], axis=1)


def write(ref, at, value):
    for c in range(ref.shape[0]):
        ref[c, at, :] = value[:, LANES * c : LANES * (c + 1)]


def decode_kernel(
    tiles, lat_ref, near_ref, far_ref, entry_ref, gain_ref, residual_ref, upscale_ref, out_hbm,
    wide, dec, hid, taps, ref, centre, slope, mix, out_ref, sems,
):
    at_ref = position()
    tile = 16
    channels = out_hbm.shape[-1]
    pitch = 24
    f32, bf16 = jnp.float32, jnp.bfloat16
    rows = tile + 4
    odd = at_ref[4] == 1
    spot = lax.broadcasted_iota(jnp.int32, (2 * pitch, 1), 0) % pitch

    def real(at, axis):
        return (at >= 0) & (at < tile * tiles[axis])

    for i in range(2 * (tile + 6)):
        if i < 2 * WIDE:
            line = jnp.where(odd, near_ref[i], far_ref[i])
        elif i < 2 * (tile + WIDE):
            line = lat_ref[i - 2 * WIDE]
        else:
            line = i - 2 * (tile + WIDE)
            line = jnp.where(odd, far_ref[line], near_ref[line])
        block = [line[dx : dx + pitch] for dx in range(3)]
        wide[pitch * i : pitch * (i + 1)] = jnp.concatenate(block, axis=1).astype(bf16)

    across = real(at_ref[1] * tile - 2 + spot, 1)
    gain = gain_ref[...]
    for y in range(rows):
        at = 2 * pitch * y
        value = jnp.dot(wide[at : at + 2 * pitch], entry_ref[0], preferred_element_type=f32)
        for dy in (1, 2):
            start = at + 2 * pitch * dy
            value += jnp.dot(wide[start : start + 2 * pitch], entry_ref[dy], preferred_element_type=f32)
        value = value.astype(bf16).astype(f32)
        write(dec, pl.ds(at, 2 * pitch), value)
        mean = jnp.mean(value * value, axis=1, keepdims=True)
        scaled = value * lax.rsqrt(mean + NORM_EPS) * gain
        active = 0.5 * scaled * (1.0 + jnp.tanh(0.5 * scaled))
        keep = across & real(at_ref[0] * tile - 2 + y, 0)
        write(hid, pl.ds(at, 2 * pitch), jnp.where(keep, active, 0.0))
    spare = jnp.zeros((8 * pitch, channels), f32)
    write(hid, pl.ds(2 * pitch * rows, 8 * pitch), spare)
    write(dec, pl.ds(2 * pitch * rows, 8 * pitch), spare)

    inner = 2 * (tile + 2)
    main = inner * tile
    edge = 40
    for i in range(2 * rows):
        for dx in range(3):
            piece = read(hid, pl.ds(pitch * i + dx, tile)).astype(bf16)
            for dy in range(3):
                j = i - 2 * dy
                if 0 <= j < inner:
                    tap = (3 * dy + dx) * channels
                    taps[tile * j : tile * (j + 1), tap : tap + channels] = piece
    for dy in range(3):
        for x in range(tile, tile + 4):
            piece = read(hid, pl.ds(2 * pitch * dy + x, edge, stride=pitch)).astype(bf16)
            for e in range(2):
                dx = x - tile - e
                if 0 <= dx < 3:
                    tap = (3 * dy + dx) * channels
                    taps[main + edge * e : main + edge * (e + 1), tap : tap + channels] = piece

    conv = jnp.dot(taps[...], residual_ref[...], preferred_element_type=f32)
    column = real(at_ref[1] * tile - 1 + lax.broadcasted_iota(jnp.int32, (tile, 1), 0), 1)
    for i in range(inner):
        value = conv[tile * i : tile * (i + 1)] + read(dec, pl.ds(pitch * (i + 2) + 1, tile))
        keep = column & real(at_ref[0] * tile - 1 + i // 2, 0)
        write(ref, pl.ds(pitch * i, tile), jnp.where(keep, value, 0.0).astype(bf16).astype(f32))
    line = real(at_ref[0] * tile - 1 + lax.broadcasted_iota(jnp.int32, (edge, 1), 0) // 2, 0)
    for e in range(2):
        value = conv[main + edge * e : main + edge * (e + 1)]
        value += read(dec, pl.ds(2 * pitch + tile + 1 + e, edge, stride=pitch))
        keep = line & real(at_ref[1] * tile - 1 + tile + e, 1)
        value = jnp.where(keep, value, 0.0).astype(bf16).astype(f32)
        write(ref, pl.ds(tile + e, edge, stride=pitch), value)

    def column_parts(i):
        left, here, right = (read(ref, pl.ds(pitch * i + d, tile)) for d in range(3))
        return left - here, here, right - here

    for image in range(2):
        before = column_parts(image)
        for y in range(tile + 1):
            after = column_parts(2 * (y + 1) + image)
            at = tile * (2 * y + image)
            for q in range(3):
                slope[q, at : at + tile] = (before[q] - after[q]).astype(bf16)
                if y < tile:
                    centre[q, at : at + tile] = after[q].astype(bf16)
            before = after

    total = 2 * tile * tile

    def product(p, q):
        source = centre[q] if p == 1 else slope[q, tile * p : tile * p + total]
        return jnp.dot(source, upscale_ref[3 * p + q], preferred_element_type=f32)

    middle = product(1, 1)
    stores = []
    shared = (middle + product(1, 0), middle + product(1, 2))
    for a in range(2):
        between = product(2 * a, 1)
        for b in range(2):
            value = shared[b] + between + product(2 * a, 2 * b)
            write(mix.at[a], pl.ds(b, total, stride=2), value)
        for y in range(tile):
            for image in range(2):
                at = 2 * tile * (2 * y + image)
                out_ref[a, image, y] = read(mix.at[a], pl.ds(at, 2 * tile)).astype(bf16)
        stores.append(pltpu.make_async_copy(out_ref.at[a], out_hbm.at[:, :, a], sems.at[a]))
        stores[a].start()
    for store in stores:
        store.wait()


def keep_kernel(source_hbm, out_ref, sems):
    parts = sems.shape[0]
    size = source_hbm.shape[0] // parts
    copies = []
    for n in range(parts):
        at = pl.ds(n * size, size)
        copies.append(pltpu.make_async_copy(source_hbm.at[at], out_ref.at[at], sems.at[n]))
        copies[n].start()
    for copy in copies:
        copy.wait()


def keep(value):
    return pl.pallas_call(
        keep_kernel,
        out_shape=pltpu.VMEM(value.shape, value.dtype),
        in_specs=[pl.BlockSpec(memory_space=pl.ANY)],
        out_specs=pl.BlockSpec(memory_space=pltpu.VMEM),
        scratch_shapes=[pltpu.SemaphoreType.DMA((4,))],
        compiler_params=pltpu.CompilerParams(vmem_limit_bytes=16 << 20),
        cost_estimate=pl.CostEstimate(flops=0, bytes_accessed=2 * value.size, transcendentals=0),
        name="keep",
    )(value)


def phases_kernel(w_hbm, out_ref, w_ref, sems):
    parts = sems.shape[0]
    size = w_hbm.shape[1] // parts
    copies = []
    for n in range(parts):
        at = pl.ds(n * size, size)
        copies.append(pltpu.make_async_copy(w_hbm.at[:, at], w_ref.at[:, at], sems.at[n]))
        copies[n].start()
    for n in range(parts):
        copies[n].wait()
        at = pl.ds(n * size, size)
        wide = [w_ref[t, at].astype(jnp.float32) for t in range(9)]
        down = [
            [wide[q], wide[q] + wide[3 + q] + wide[6 + q], -wide[6 + q]] for q in range(3)
        ]
        for p in range(3):
            left, middle, right = (down[q][p] for q in range(3))
            out_ref[3 * p, at] = left.astype(jnp.bfloat16)
            out_ref[3 * p + 1, at] = (left + middle + right).astype(jnp.bfloat16)
            out_ref[3 * p + 2, at] = right.astype(jnp.bfloat16)


def phases(upscale):
    deep, channels = upscale.shape[2:]
    shape = (9, deep, channels)
    return pl.pallas_call(
        phases_kernel,
        out_shape=pltpu.VMEM(shape, jnp.bfloat16),
        in_specs=[pl.BlockSpec(memory_space=pl.ANY)],
        out_specs=pl.BlockSpec(memory_space=pltpu.VMEM),
        scratch_shapes=[pltpu.VMEM(shape, jnp.bfloat16), pltpu.SemaphoreType.DMA((8,))],
        compiler_params=pltpu.CompilerParams(vmem_limit_bytes=32 << 20),
        cost_estimate=pl.CostEstimate(flops=10 * deep * channels, bytes_accessed=18 * deep * channels, transcendentals=0),
        name="phases",
    )(upscale.reshape(shape))


def decode(latent, entry, gain, residual, combined, tiles):
    images, tile = 2, 16
    latents = latent[0].shape[-1]
    channels = entry.shape[-1]
    pitch = 24
    rows = images * (tile + 4) + 8
    inner = images * (tile + 2)
    total = images * tile * tile
    f32, bf16 = jnp.float32, jnp.bfloat16
    vmem = pl.BlockSpec(memory_space=pltpu.VMEM)
    hbm = pl.BlockSpec(memory_space=pl.ANY)
    out = pl.pallas_call(
        functools.partial(decode_kernel, tiles),
        out_shape=jax.ShapeDtypeStruct((images, tile, 2, 2 * tile, channels), bf16),
        in_specs=[vmem] * 7,
        out_specs=hbm,
        scratch_shapes=[
            pltpu.VMEM((images * (tile + 6) * pitch, 3 * latents), bf16),
            pltpu.VMEM((channels // LANES, rows * pitch, LANES), f32),
            pltpu.VMEM((channels // LANES, rows * pitch, LANES), f32),
            pltpu.VMEM((inner * tile + 80, 9 * channels), bf16),
            pltpu.VMEM((channels // LANES, (inner + 4) * pitch, LANES), f32),
            pltpu.VMEM((3, total, channels), bf16),
            pltpu.VMEM((3, total + images * tile, channels), bf16),
            pltpu.VMEM((2, channels // LANES, 2 * total, LANES), f32),
            pltpu.VMEM((2, images, tile, 2 * tile, channels), bf16),
            pltpu.SemaphoreType.DMA((2,)),
        ],
        compiler_params=pltpu.CompilerParams(vmem_limit_bytes=40 << 20),
        cost_estimate=pl.CostEstimate(flops=8 * 10**9, bytes_accessed=12 << 20, transcendentals=0),
        name="decode",
    )(
        *latent,
        entry.reshape(3, 3 * entry.shape[2], channels),
        gain.reshape(1, channels),
        residual,
        combined,
    )
    return out.reshape(images, 2 * tile, 2 * tile, channels)


def local(
    queries,
    key_rows_per_head,
    value_rows_per_head,
    latent_projection_weight,
    entry_conv_weight,
    residual_norm_gain,
    residual_conv_weight,
    upscale_conv_weight,
):
    images, tile, _, width = queries.shape
    scale = 1.0 / (tile * lax.axis_size("row") * tile * lax.axis_size("col"))
    flat = (images, tile * tile, width)
    keys, values = key_rows_per_head.reshape(flat), value_rows_per_head.reshape(flat)
    mine, other = image_sums(keys, values, scale)
    channels = residual_conv_weight.shape[-1]
    residual = residual_conv_weight.reshape(9 * channels, channels)
    queries = queries.reshape(flat)
    pieces, beside, residual, combined = gather_all(
        mine, other, queries, residual, upscale_conv_weight
    )
    latent, near, far = attend(queries, beside, pieces, latent_projection_weight)
    near, far = swapped(near, far, "row")
    return decode(
        (latent, near, far),
        entry_conv_weight,
        residual_norm_gain,
        residual,
        combined,
        (lax.axis_size("row"), lax.axis_size("col")),
    )


def solution(mesh):
    placed = (
        P(None, "row", "col", None),
        P(None, "row", "col", None),
        P(None, "row", "col", None),
        P(),
        P(),
        P(),
        P(),
        P(),
    )
    return jax.shard_map(
        local, mesh=mesh, in_specs=placed, out_specs=P(None, "row", "col", None), check_vma=False
    )
```

```python
import functools

import jax
import jax.numpy as jnp
from jax import lax
from jax.experimental import pallas as pl
from jax.experimental.pallas import tpu as pltpu
from jax.sharding import PartitionSpec as P

HEAD = 32
NORM_EPS = 1e-06
LANES = 128
PACK = 2560
KS_AT = 2304
WIDE = 3
SPLIT = (1, 3, 2)


def position():
    row, col = lax.axis_index("row"), lax.axis_index("col")
    return row, col, lax.rem(row, 4), lax.rem(col, 2), lax.rem(row, 2)


def sums_kernel(scale, k_hbm, v_hbm, mine_ref, other_ref, k_ref, v_ref, sems):
    images, tokens, width = k_ref.shape
    core = position()[3]
    half = tokens // 2
    copies = []
    for n in range(images):
        image = 1 - core if n == 0 else core
        for c in range(2):
            at = pl.ds(half * c, half)
            for m, (source, target) in enumerate(((k_hbm, k_ref), (v_hbm, v_ref))):
                copies.append(
                    pltpu.make_async_copy(source.at[image, at], target.at[n, at], sems.at[n, c, m])
                )
    for copy in copies:
        copy.start()
    ones = jnp.ones((tokens, LANES), jnp.bfloat16)
    lane = lax.broadcasted_iota(jnp.int32, (HEAD, LANES), 1)
    for n, out_ref in ((0, other_ref), (1, mine_ref)):
        for copy in copies[4 * n : 4 * n + 4]:
            copy.wait()
        parts = []
        key_sums = jnp.zeros((HEAD, LANES), jnp.float32)
        for start in range(0, width, LANES):
            size = min(LANES, width - start)
            keys = jnp.maximum(k_ref[n, :, start : start + size], 0)
            values = jnp.concatenate([v_ref[n, :, start : start + size], ones], axis=1)
            product = lax.dot_general(
                keys, values, (((0,), (0,)), ((), ())), preferred_element_type=jnp.float32
            )
            packed = jnp.zeros((HEAD, size), jnp.float32)
            for h in range(size // HEAD):
                rows = product[h * HEAD : (h + 1) * HEAD]
                packed = jnp.where(lane[:, :size] // HEAD == h, rows[:, :size], packed)
                key_sums = jnp.where(lane == start // HEAD + h, rows[:, size:], key_sums)
            parts.append(packed)
        parts.append(jnp.zeros((HEAD, KS_AT - width), jnp.float32))
        parts.append(key_sums)
        parts.append(jnp.zeros((HEAD, PACK - KS_AT - LANES), jnp.float32))
        total = (jnp.concatenate(parts, axis=1) * scale).astype(jnp.bfloat16)
        wide = PACK // 2
        for r in range(2):
            for c in range(2):
                out_ref[2 * r + c] = total[16 * r : 16 * r + 16, wide * c : wide * (c + 1)]


def image_sums(keys, values, scale):
    images, tokens, width = keys.shape
    out = pltpu.VMEM((4, 16, PACK // 2), jnp.bfloat16)
    vmem = pl.BlockSpec(memory_space=pltpu.VMEM)
    hbm = pl.BlockSpec(memory_space=pl.ANY)
    return pl.pallas_call(
        functools.partial(sums_kernel, scale),
        out_shape=[out, out],
        in_specs=[hbm, hbm],
        out_specs=[vmem, vmem],
        scratch_shapes=[
            pltpu.VMEM(keys.shape, keys.dtype),
            pltpu.VMEM(values.shape, values.dtype),
            pltpu.SemaphoreType.DMA((images, 2, 2)),
        ],
        compiler_params=pltpu.CompilerParams(vmem_limit_bytes=56 << 20),
        cost_estimate=pl.CostEstimate(flops=4 * tokens * width * 256, bytes_accessed=8 * tokens * width, transcendentals=0),
        name="image_sums",
    )(keys, values)


def sides_kernel(q_ref, near_ref, far_ref):
    at_ref = position()
    tokens = q_ref.shape[1]
    edge = near_ref.shape[1]
    odd = at_ref[3] == 1
    side = 16
    row = lax.broadcasted_iota(jnp.int32, (2 * edge, tokens), 0)
    column = lax.broadcasted_iota(jnp.int32, (2 * edge, tokens), 1)
    place = row % edge
    wanted = side * (place // WIDE) + place % WIDE + (row // edge) * (side - WIDE)
    pick = (column == wanted).astype(jnp.bfloat16)
    picked = jnp.dot(pick, q_ref[0], preferred_element_type=jnp.float32).astype(jnp.bfloat16)
    near_ref[0] = jnp.where(odd, picked[:edge], picked[edge:])
    far_ref[0] = jnp.where(odd, picked[edge:], picked[:edge])


def sides(queries):
    images, tokens, width = queries.shape
    edge = 16 * WIDE
    out = jax.ShapeDtypeStruct((images, edge, width), queries.dtype)
    block = pl.BlockSpec((1, edge, width), lambda i: (i, 0, 0))
    return pl.pallas_call(
        sides_kernel,
        out_shape=[out, out],
        grid=(images,),
        in_specs=[pl.BlockSpec((1, tokens, width), lambda i: (i, 0, 0))],
        out_specs=[block, block],
        compiler_params=pltpu.CompilerParams(vmem_limit_bytes=48 << 20),
        cost_estimate=pl.CostEstimate(flops=10**9, bytes_accessed=3 * images * tokens * width, transcendentals=0),
        name="sides",
    )(queries)


def attend_kernel(
    q_ref, near_ref, far_ref, *rest,
):
    at_ref = position()
    pieces, (weight_ref, out_ref, near_out_ref, far_out_ref, sums) = rest[:8], rest[8:]
    f32, bf16 = jnp.float32, jnp.bfloat16
    images, inner, width = q_ref.shape
    edge = near_ref.shape[1]
    odd = at_ref[3] == 1
    odd_row = at_ref[4] == 1
    tokens = inner + 2 * edge
    tile = 16
    group = 2 * LANES
    for n in range(4):
        sums[at_ref[2] ^ n, at_ref[3]] = pieces[n][...]
        sums[at_ref[2] ^ n, 1 - at_ref[3]] = pieces[4 + n][...]
    same = (
        lax.broadcasted_iota(jnp.int32, (group, group), 0) // HEAD
        == lax.broadcasted_iota(jnp.int32, (group, group), 1) // HEAD
    )
    same = same.astype(f32).astype(bf16)
    head_of = lax.broadcasted_iota(jnp.int32, (LANES, PACK), 0)
    lane_head = lax.broadcasted_iota(jnp.int32, (LANES, PACK), 1) // HEAD
    spread = (head_of == lane_head).astype(f32).astype(bf16)
    kv = [
        jnp.concatenate(
            [jnp.concatenate([sums[2 * r + c, image] for c in range(2)], axis=1) for r in range(2)], axis=0
        )
        for image in range(images)
    ]
    key_means = jnp.concatenate([part[:, KS_AT : KS_AT + LANES] for part in kv], axis=0)
    means = jnp.dot(key_means, spread, preferred_element_type=f32).astype(bf16)
    squares = [jnp.zeros((tokens, LANES), f32)] * images
    latent = jnp.zeros((images * tokens, weight_ref.shape[0]), f32)
    for start in range(0, width, group):
        size = min(group, width - start)
        repeat = size // HEAD
        here = same[:size, :size]
        parts = []
        for image in range(images):
            upper = kv[image][:, start : start + size]
            lower = means[HEAD * image : HEAD * (image + 1), start : start + size]
            lanes = slice(start, start + size)
            near, far = near_ref[image, :, lanes], far_ref[image, :, lanes]
            query = [q_ref[image, :, lanes], jnp.where(odd, near, far), jnp.where(odd, far, near)]
            query = jnp.maximum(jnp.concatenate(query, axis=0), 0)
            numerator = jnp.dot(
                query, jnp.concatenate([upper] * repeat, axis=0) * here, preferred_element_type=f32
            )
            denominator = jnp.dot(
                query, jnp.concatenate([lower] * repeat, axis=0) * here, preferred_element_type=f32
            )
            attended = numerator * pl.reciprocal(jnp.maximum(denominator, 1.0), approx=True)
            square = attended * attended
            for c in range(0, size, LANES):
                part = square[:, c : min(c + LANES, size)]
                if part.shape[1] < LANES:
                    rest = jnp.zeros((tokens, LANES - part.shape[1]), f32)
                    part = jnp.concatenate([part, rest], axis=1)
                squares[image] += part
            parts.append(attended.astype(bf16))
        latent += lax.dot_general(
            jnp.concatenate(parts, axis=0),
            weight_ref[:, start : start + size],
            (((1,), (1,)), ((), ())),
            preferred_element_type=f32,
        )
    for image in range(images):
        total = jnp.sum(squares[image], axis=1, keepdims=True)
        normed = latent[tokens * image : tokens * (image + 1)] * lax.rsqrt(total / width + NORM_EPS)
        normed = normed.astype(bf16).astype(f32)
        for y in range(tile):
            line = images * y + image
            at = inner + WIDE * y
            out_ref[line, :WIDE] = normed[at : at + WIDE]
            out_ref[line, WIDE : WIDE + tile] = normed[tile * y : tile * (y + 1)]
            at += edge
            out_ref[line, WIDE + tile : 2 * WIDE + tile] = normed[at : at + WIDE]
    out_ref[:, 2 * WIDE + tile :] = jnp.zeros((images * tile, 10, weight_ref.shape[0]), f32)
    first = out_ref[: images * WIDE].astype(bf16)
    last = out_ref[images * (tile - WIDE) :].astype(bf16)
    near_out_ref[...] = jnp.where(odd_row, first, last)
    far_out_ref[...] = jnp.where(odd_row, last, first)


def attend(queries, sides, pieces, weight):
    images, tokens, width = queries.shape
    channels = weight.shape[1]
    vmem = pl.BlockSpec(memory_space=pltpu.VMEM)
    return pl.pallas_call(
        attend_kernel,
        out_shape=[
            jax.ShapeDtypeStruct((images * lines, 32, channels), kind)
            for lines, kind in ((16, jnp.float32), (WIDE, jnp.bfloat16), (WIDE, jnp.bfloat16))
        ],
        in_specs=[vmem] * 12,
        out_specs=[vmem] * 3,
        scratch_shapes=[pltpu.VMEM((4, images, 16, PACK // 2), jnp.bfloat16)],
        compiler_params=pltpu.CompilerParams(vmem_limit_bytes=32 << 20),
        cost_estimate=pl.CostEstimate(flops=2 * images * tokens * width * 512, bytes_accessed=2 * images * tokens * width, transcendentals=0),
        name="attend",
    )(queries, *sides, *pieces, weight.T)


def xor_pairs(distance):
    return [(i, i ^ distance) for i in range(16)]


def added(value, arrived):
    total = value.astype(jnp.float32)
    for part in arrived:
        total = total + part.astype(jnp.float32)
    return total.astype(jnp.bfloat16)


def sent(value, axis, distances):
    return [lax.ppermute(value, axis, xor_pairs(d)) for d in distances]


def swapped(even, odd, axis):
    size = lax.axis_size(axis)
    near = [(i, i ^ 1) for i in range(size)]
    far = [(i, i - 1 if i % 2 == 0 else i + 1) for i in range(1, size - 1)]
    return lax.ppermute(even, axis, near), lax.ppermute(odd, axis, far)


def split_kernel(mine_ref, arrived_ref, own_ref, *parts_ref):
    at_ref = position()
    f32 = jnp.float32
    for d, out_ref in zip((0,) + SPLIT, (own_ref,) + parts_ref):
        chunk = at_ref[2] ^ d
        total = mine_ref[chunk].astype(f32) + arrived_ref[chunk].astype(f32)
        out_ref[...] = total.astype(out_ref.dtype)


def split(mine, arrived):
    shape = mine.shape[1:]
    vmem = pl.BlockSpec(memory_space=pltpu.VMEM)
    return pl.pallas_call(
        split_kernel,
        out_shape=[jax.ShapeDtypeStruct(shape, jnp.float32)]
        + [jax.ShapeDtypeStruct(shape, jnp.bfloat16)] * len(SPLIT),
        in_specs=[vmem, vmem],
        out_specs=[vmem] * (1 + len(SPLIT)),
        compiler_params=pltpu.CompilerParams(vmem_limit_bytes=8 << 20),
        name="split",
    )(mine, arrived)


def gather_all(mine, other, queries, residual, upscale):
    hold = lax.optimization_barrier
    arrived = lax.ppermute(other, "col", xor_pairs(1))
    near, mine = hold((queries, mine))
    start, end = sides(near)
    arrived, start, end = hold((arrived, start, end))
    own, *parts = split(mine, arrived)
    parts = [lax.ppermute(part, "row", xor_pairs(d)) for part, d in zip(parts, SPLIT)]
    chunk = added(own, parts)

    chunk, weights, start, end = hold((chunk, residual, start, end))
    arrived = sent(chunk, "row", (4, 12, 8))
    beside = swapped(start, end, "col")
    arrived, kept = hold((arrived, keep(weights)))
    chunk = added(chunk, arrived)

    chunk = added(chunk, sent(chunk, "col", (2,)))

    chunk, weights = hold((chunk, upscale))
    arrived = sent(chunk, "col", (4, 12, 10))
    arrived, combined = hold((arrived, phases(weights)))
    chunk = added(chunk, arrived)

    pieces = [chunk] + sent(chunk, "row", (1, 2, 3))
    pieces += [lax.ppermute(piece, "col", xor_pairs(1)) for piece in pieces]
    return pieces, beside, kept, combined


def read(ref, at):
    return jnp.concatenate([ref[c, at, :] for c in range(ref.shape[0])], axis=1)


def write(ref, at, value):
    for c in range(ref.shape[0]):
        ref[c, at, :] = value[:, LANES * c : LANES * (c + 1)]


def decode_kernel(
    tiles, lat_ref, near_ref, far_ref, entry_ref, gain_ref, residual_ref, upscale_ref, out_hbm,
    wide, dec, hid, taps, ref, centre, slope, mix, out_ref, sems,
):
    at_ref = position()
    tile = 16
    channels = out_hbm.shape[-1]
    pitch = 24
    f32, bf16 = jnp.float32, jnp.bfloat16
    rows = tile + 4
    odd = at_ref[4] == 1
    spot = lax.broadcasted_iota(jnp.int32, (2 * pitch, 1), 0) % pitch

    def real(at, axis):
        return (at >= 0) & (at < tile * tiles[axis])

    for i in range(2 * (tile + 6)):
        if i < 2 * WIDE:
            line = jnp.where(odd, near_ref[i], far_ref[i]).astype(f32)
        elif i < 2 * (tile + WIDE):
            line = lat_ref[i - 2 * WIDE]
        else:
            line = i - 2 * (tile + WIDE)
            line = jnp.where(odd, far_ref[line], near_ref[line]).astype(f32)
        block = [line[dx : dx + pitch] for dx in range(3)]
        wide[pitch * i : pitch * (i + 1)] = jnp.concatenate(block, axis=1).astype(bf16)

    across = real(at_ref[1] * tile - 2 + spot, 1)
    gain = gain_ref[...]
    for y in range(rows):
        at = 2 * pitch * y
        value = jnp.dot(wide[at : at + 2 * pitch], entry_ref[0], preferred_element_type=f32)
        for dy in (1, 2):
            start = at + 2 * pitch * dy
            value += jnp.dot(wide[start : start + 2 * pitch], entry_ref[dy], preferred_element_type=f32)
        value = value.astype(bf16).astype(f32)
        write(dec, pl.ds(at, 2 * pitch), value)
        mean = jnp.mean(value * value, axis=1, keepdims=True)
        scaled = value * lax.rsqrt(mean + NORM_EPS) * gain
        active = 0.5 * scaled * (1.0 + jnp.tanh(0.5 * scaled))
        keep = across & real(at_ref[0] * tile - 2 + y, 0)
        write(hid, pl.ds(at, 2 * pitch), jnp.where(keep, active, 0.0))
    spare = jnp.zeros((8 * pitch, channels), f32)
    write(hid, pl.ds(2 * pitch * rows, 8 * pitch), spare)
    write(dec, pl.ds(2 * pitch * rows, 8 * pitch), spare)

    inner = 2 * (tile + 2)
    main = inner * tile
    edge = 40
    for i in range(2 * rows):
        for dx in range(3):
            piece = read(hid, pl.ds(pitch * i + dx, tile)).astype(bf16)
            for dy in range(3):
                j = i - 2 * dy
                if 0 <= j < inner:
                    tap = (3 * dy + dx) * channels
                    taps[tile * j : tile * (j + 1), tap : tap + channels] = piece
    for dy in range(3):
        for x in range(tile, tile + 4):
            piece = read(hid, pl.ds(2 * pitch * dy + x, edge, stride=pitch)).astype(bf16)
            for e in range(2):
                dx = x - tile - e
                if 0 <= dx < 3:
                    tap = (3 * dy + dx) * channels
                    taps[main + edge * e : main + edge * (e + 1), tap : tap + channels] = piece

    conv = jnp.dot(taps[...], residual_ref[...], preferred_element_type=f32)
    column = real(at_ref[1] * tile - 1 + lax.broadcasted_iota(jnp.int32, (tile, 1), 0), 1)
    for i in range(inner):
        value = conv[tile * i : tile * (i + 1)] + read(dec, pl.ds(pitch * (i + 2) + 1, tile))
        keep = column & real(at_ref[0] * tile - 1 + i // 2, 0)
        write(ref, pl.ds(pitch * i, tile), jnp.where(keep, value, 0.0).astype(bf16).astype(f32))
    line = real(at_ref[0] * tile - 1 + lax.broadcasted_iota(jnp.int32, (edge, 1), 0) // 2, 0)
    for e in range(2):
        value = conv[main + edge * e : main + edge * (e + 1)]
        value += read(dec, pl.ds(2 * pitch + tile + 1 + e, edge, stride=pitch))
        keep = line & real(at_ref[1] * tile - 1 + tile + e, 1)
        value = jnp.where(keep, value, 0.0).astype(bf16).astype(f32)
        write(ref, pl.ds(tile + e, edge, stride=pitch), value)

    def column_parts(i):
        left, here, right = (read(ref, pl.ds(pitch * i + d, tile)) for d in range(3))
        return left - here, here, right - here

    for image in range(2):
        before = column_parts(image)
        for y in range(tile + 1):
            after = column_parts(2 * (y + 1) + image)
            at = tile * (2 * y + image)
            for q in range(3):
                slope[q, at : at + tile] = (before[q] - after[q]).astype(bf16)
                if y < tile:
                    centre[q, at : at + tile] = after[q].astype(bf16)
            before = after

    total = 2 * tile * tile

    def product(p, q):
        source = centre[q] if p == 1 else slope[q, tile * p : tile * p + total]
        return jnp.dot(source, upscale_ref[3 * p + q], preferred_element_type=f32)

    middle = product(1, 1)
    stores = []
    shared = (middle + product(1, 0), middle + product(1, 2))
    for a in range(2):
        between = product(2 * a, 1)
        for b in range(2):
            value = shared[b] + between + product(2 * a, 2 * b)
            write(mix.at[a], pl.ds(b, total, stride=2), value)
        for y in range(tile):
            for image in range(2):
                at = 2 * tile * (2 * y + image)
                out_ref[a, image, y] = read(mix.at[a], pl.ds(at, 2 * tile)).astype(bf16)
        stores.append(pltpu.make_async_copy(out_ref.at[a], out_hbm.at[:, :, a], sems.at[a]))
        stores[a].start()
    for store in stores:
        store.wait()


def keep_kernel(source_hbm, out_ref, sems):
    parts = sems.shape[0]
    size = source_hbm.shape[0] // parts
    copies = []
    for n in range(parts):
        at = pl.ds(n * size, size)
        copies.append(pltpu.make_async_copy(source_hbm.at[at], out_ref.at[at], sems.at[n]))
        copies[n].start()
    for copy in copies:
        copy.wait()


def keep(value):
    return pl.pallas_call(
        keep_kernel,
        out_shape=pltpu.VMEM(value.shape, value.dtype),
        in_specs=[pl.BlockSpec(memory_space=pl.ANY)],
        out_specs=pl.BlockSpec(memory_space=pltpu.VMEM),
        scratch_shapes=[pltpu.SemaphoreType.DMA((4,))],
        compiler_params=pltpu.CompilerParams(vmem_limit_bytes=16 << 20),
        cost_estimate=pl.CostEstimate(flops=0, bytes_accessed=2 * value.size, transcendentals=0),
        name="keep",
    )(value)


def phases_kernel(w_hbm, out_ref, w_ref, sems):
    parts = sems.shape[0]
    size = w_hbm.shape[1] // parts
    copies = []
    for n in range(parts):
        at = pl.ds(n * size, size)
        copies.append(pltpu.make_async_copy(w_hbm.at[:, at], w_ref.at[:, at], sems.at[n]))
        copies[n].start()
    for n in range(parts):
        copies[n].wait()
        at = pl.ds(n * size, size)
        wide = [w_ref[t, at].astype(jnp.float32) for t in range(9)]
        down = [
            [wide[q], wide[q] + wide[3 + q] + wide[6 + q], -wide[6 + q]] for q in range(3)
        ]
        for p in range(3):
            left, middle, right = (down[q][p] for q in range(3))
            out_ref[3 * p, at] = left.astype(jnp.bfloat16)
            out_ref[3 * p + 1, at] = (left + middle + right).astype(jnp.bfloat16)
            out_ref[3 * p + 2, at] = right.astype(jnp.bfloat16)


def phases(upscale):
    deep, channels = upscale.shape[2:]
    shape = (9, deep, channels)
    return pl.pallas_call(
        phases_kernel,
        out_shape=pltpu.VMEM(shape, jnp.bfloat16),
        in_specs=[pl.BlockSpec(memory_space=pl.ANY)],
        out_specs=pl.BlockSpec(memory_space=pltpu.VMEM),
        scratch_shapes=[pltpu.VMEM(shape, jnp.bfloat16), pltpu.SemaphoreType.DMA((8,))],
        compiler_params=pltpu.CompilerParams(vmem_limit_bytes=32 << 20),
        cost_estimate=pl.CostEstimate(flops=10 * deep * channels, bytes_accessed=18 * deep * channels, transcendentals=0),
        name="phases",
    )(upscale.reshape(shape))


def decode(latent, entry, gain, residual, combined, tiles):
    images, tile = 2, 16
    latents = latent[0].shape[-1]
    channels = entry.shape[-1]
    pitch = 24
    rows = images * (tile + 4) + 8
    inner = images * (tile + 2)
    total = images * tile * tile
    f32, bf16 = jnp.float32, jnp.bfloat16
    vmem = pl.BlockSpec(memory_space=pltpu.VMEM)
    hbm = pl.BlockSpec(memory_space=pl.ANY)
    out = pl.pallas_call(
        functools.partial(decode_kernel, tiles),
        out_shape=jax.ShapeDtypeStruct((images, tile, 2, 2 * tile, channels), bf16),
        in_specs=[vmem] * 7,
        out_specs=hbm,
        scratch_shapes=[
            pltpu.VMEM((images * (tile + 6) * pitch, 3 * latents), bf16),
            pltpu.VMEM((channels // LANES, rows * pitch, LANES), f32),
            pltpu.VMEM((channels // LANES, rows * pitch, LANES), f32),
            pltpu.VMEM((inner * tile + 80, 9 * channels), bf16),
            pltpu.VMEM((channels // LANES, (inner + 4) * pitch, LANES), f32),
            pltpu.VMEM((3, total, channels), bf16),
            pltpu.VMEM((3, total + images * tile, channels), bf16),
            pltpu.VMEM((2, channels // LANES, 2 * total, LANES), f32),
            pltpu.VMEM((2, images, tile, 2 * tile, channels), bf16),
            pltpu.SemaphoreType.DMA((2,)),
        ],
        compiler_params=pltpu.CompilerParams(vmem_limit_bytes=40 << 20),
        cost_estimate=pl.CostEstimate(flops=8 * 10**9, bytes_accessed=12 << 20, transcendentals=0),
        name="decode",
    )(
        *latent,
        entry.reshape(3, 3 * entry.shape[2], channels),
        gain.reshape(1, channels),
        residual,
        combined,
    )
    return out.reshape(images, 2 * tile, 2 * tile, channels)


def local(
    queries,
    key_rows_per_head,
    value_rows_per_head,
    latent_projection_weight,
    entry_conv_weight,
    residual_norm_gain,
    residual_conv_weight,
    upscale_conv_weight,
):
    images, tile, _, width = queries.shape
    scale = 1.0 / (tile * lax.axis_size("row") * tile * lax.axis_size("col"))
    flat = (images, tile * tile, width)
    keys, values = key_rows_per_head.reshape(flat), value_rows_per_head.reshape(flat)
    mine, other = image_sums(keys, values, scale)
    channels = residual_conv_weight.shape[-1]
    residual = residual_conv_weight.reshape(9 * channels, channels)
    queries = queries.reshape(flat)
    pieces, beside, residual, combined = gather_all(
        mine, other, queries, residual, upscale_conv_weight
    )
    latent, near, far = attend(queries, beside, pieces, latent_projection_weight)
    near, far = swapped(near, far, "row")
    return decode(
        (latent, near, far),
        entry_conv_weight,
        residual_norm_gain,
        residual,
        combined,
        (lax.axis_size("row"), lax.axis_size("col")),
    )


def solution(mesh):
    placed = (
        P(None, "row", "col", None),
        P(None, "row", "col", None),
        P(None, "row", "col", None),
        P(),
        P(),
        P(),
        P(),
        P(),
    )
    return jax.shard_map(
        local, mesh=mesh, in_specs=placed, out_specs=P(None, "row", "col", None), check_vma=False
    )
```
